512 devices in a mesh: shot: 8 (over z_lo), slab: 64 (over x, z_hi, y, core).
Axes of the slice: x: 4, y: 4, z: 16 (z_hi: 2, z_lo: 8; z = z_hi * 8 + z_lo), core: 2. Of those that a mesh axis runs over, the one named last changes fastest.
Arguments:
- partial_grads: bfloat16 [8, 3, 1024, 128, 256], P('shot', None, 'slab'), may hold values from -6 to 6
- model: float32 [3, 1024, 128, 256], P(None, 'slab', 'shot'), may hold values from 0.8 to 1.6
- tilt: float32 [1024, 128, 256], P('slab', 'shot'), may hold values from -3.140625 to 3.140625
- widths: float32 [3, 1024], replicated, may hold values from 2 to 64
- step_length: float32 [3], replicated, may hold values from 0.1 to 0.4
Outputs:
- coefficients: float32 [3, 1024, 128, 256], P(None, 'slab', 'shot')
The draws below stay inside these ranges and needn't reach their ends.
All inputs are finite; a program needn't handle non-finite values.
Results may differ from the reference program's by a relative error of at most 0.004.
Values may be sent and summed in bfloat16 or wider, within the bound.
A program may use at most 64 MiB of HBM per device.

```python
import math
import jax
import jax.numpy as jnp

NZ = 1024
NY = 256
NX = 128
N_SHOT = 8


def with_spikes(array, own_key, source, target, blocks, factor):
    owner, partner = [(jnp.arange(array.shape[dim]) // (array.shape[dim] // blocks)).reshape([-1 if axis == dim else 1 for axis in range(array.ndim)]) for dim in (source, target)]
    chosen = jax.random.permutation(own_key, blocks)[partner]
    strong = (owner == chosen) | (owner == (partner + blocks // 2) % blocks)
    return jnp.where(strong, factor * array, array)


def block_levels(rng, dims, pieces, least, top_value):
    def one(axis_at, parts):
        steps = jax.random.uniform(jax.random.fold_in(jax.random.fold_in(rng, 6), axis_at), (parts,), jnp.float32, least / len(pieces), top_value / len(pieces))
        return jnp.repeat(jnp.exp(steps), dims[axis_at] // parts).reshape((-1,) + (1,) * (len(dims) - axis_at - 1))

    gain = one(*pieces[0])
    for cut in pieces[1:]:
        gain = gain * one(*cut)
    return gain


def bell_draw_with(rng, shape, deviation, most, cuts, heavy, kind=jnp.bfloat16):
    values = deviation * jax.random.normal(rng, shape, jnp.float32)
    if cuts:
        values = values * block_levels(rng, shape, cuts, -0.22, 0.18)
    return jnp.clip(with_spikes(values, jax.random.fold_in(rng, 3), *heavy), -most, most).astype(kind)


def setup_inputs(seed: int = 0) -> dict:
    key_of = jax.random.split(jax.random.key(seed), 6)
    partial_grads = bell_draw_with(key_of[0], (N_SHOT, 3, NZ, NX, NY), 1.0, 6.0, ((0, 8), (2, 64)), (0, 3, 8, 2.0))
    model = jnp.clip(0.8 + 0.8 * jax.random.uniform(key_of[1], (3, NZ, NX, NY), jnp.float32) ** block_levels(key_of[1], (3, NZ, NX, NY), ((1, 64), (2, 8)), -0.2, 0.2), 0.8, 1.6)
    tilt = jnp.clip(jax.random.uniform(key_of[2], (NZ, NX, NY), jnp.float32, -3.140625, 3.140625), -3.140625, 3.140625)
    widths = jnp.clip(jnp.exp(jax.random.uniform(key_of[3], (3, NZ), jnp.float32, math.log(2.0), math.log(64.0))), 2.0, 64.0)
    step_length = jnp.clip(jax.random.uniform(key_of[4], (3,), jnp.float32, 0.1, 0.4), 0.1, 0.4)
    return dict(partial_grads=partial_grads, model=model, tilt=tilt, widths=widths, step_length=step_length)


def smoother(width_row):
    depths = jnp.arange(NZ, dtype=jnp.float32)
    offset = depths[:, None] - depths[None, :]
    kernel = jnp.exp(-offset * offset / (2.0 * width_row[:, None] * width_row[:, None]))
    return (kernel / jnp.sum(kernel, axis=1, keepdims=True)).astype(jnp.bfloat16)


def rotate(velocity, epsilon, delta, angle):
    squared = velocity * velocity
    along = squared * (1.0 + 2.0 * epsilon)
    normal = squared * (1.0 + 2.0 * delta)
    cosine = jnp.cos(angle)
    sine = jnp.sin(angle)
    first = along * cosine * cosine + squared * sine * sine
    second = along * sine * sine + squared * cosine * cosine
    third = (normal - squared) * sine * cosine
    return jnp.stack([first, second, third])


def average(padded):
    depth_cells = padded.shape[1] - 2
    x_cells = padded.shape[2] - 2
    weights = [0.25, 0.5, 0.25]
    total = jnp.zeros((padded.shape[0], depth_cells, x_cells, padded.shape[3]), jnp.float32)
    for shift_z in range(3):
        for shift_x in range(3):
            total = total + (weights[shift_z] * weights[shift_x]) * padded[:, shift_z:shift_z + depth_cells, shift_x:shift_x + x_cells, :]
    return total


def reference(partial_grads, model, tilt, widths, step_length):
    gradient = jnp.sum(partial_grads.astype(jnp.float32), axis=0).astype(jnp.bfloat16)
    smoothed_list = []
    for which in range(3):
        matrix = smoother(widths[which])
        flat = gradient[which].reshape(NZ, NX * NY)
        smoothed_list.append(jnp.dot(matrix, flat, preferred_element_type=jnp.float32).astype(jnp.bfloat16).reshape(NZ, NX, NY))
    smoothed = jnp.stack(smoothed_list)
    updated = model - step_length[:, None, None, None] * smoothed.astype(jnp.float32)
    rotated = rotate(updated[0], updated[1], updated[2], tilt)
    padded = jnp.pad(rotated, ((0, 0), (1, 1), (1, 1), (0, 0)))
    return average(padded)
```

```python
import jax
import jax.numpy as jnp
from jax import lax
from jax.experimental import pallas as pl
from jax.experimental.pallas import tpu as pltpu
from jax.sharding import PartitionSpec as P

MESH = pl.DeviceIdType.MESH
F32 = jnp.float32
BF16 = jnp.bfloat16

SHOTS = 8
SLABS = 64
LAST = SHOTS - 1
ROWS = 16
HALF = 128
NZ = ROWS * SLABS
PIECE = 8
SPLIT = ROWS // PIECE
PER_PARAM = SHOTS * SPLIT
PIECES = 3 * PER_PARAM
SKEW = 4
LAG = 8
BLOCK = 256
BUILD = 128
STEPS_BUILD = 3 * NZ // BUILD


def kernel(
    grads, model, tilt, widths, step, out,
    held, turn, parts, pencil, matrix, product, back, flat, wave, rot, border, corner, side, near, edge,
    stream_send, stream_recv, part_send, part_recv, back_send, back_recv, halo_send, halo_recv,
):
    shot = lax.axis_index("shot")
    slab = lax.axis_index("slab")
    upper = (slab // 8) % 2
    rank_0 = shot + upper * (LAST - 2 * shot)
    sign_0 = 1 - 2 * upper
    ranks = (rank_0, LAST - rank_0)
    signs = (sign_0, -sign_0)
    is_end = (rank_0 == 0) | (rank_0 == LAST)
    end_half = jnp.where(rank_0 == LAST, 0, 1)
    slot_own = slab % 8
    pair_own = slab // 8
    chunk_own = slot_own // 2 + 4 * (slot_own % 2)

    has = {"low": shot > 0, "high": shot < LAST}
    deep = {"low": slab > 0, "high": slab < SLABS - 1}
    corner[...] = jnp.zeros_like(corner)

    @pl.when(jnp.logical_not(deep["low"]))
    def _():
        rot[:, :, 0:ROWS] = jnp.zeros((2, 3, ROWS, HALF), F32)

    @pl.when(jnp.logical_not(deep["high"]))
    def _():
        rot[:, :, ROWS * (ROWS + 1) :] = jnp.zeros((2, 3, ROWS, HALF), F32)

    def send_piece(src, h, k):
        pltpu.make_async_remote_copy(
            src_ref=src, dst_ref=held.at[h, k], send_sem=stream_send.at[h], recv_sem=stream_recv.at[h, k],
            device_id={"shot": shot + signs[h], "slab": slab}, device_id_type=MESH,
        ).start()

    def owner_of(h, g):
        high = (g // 8) % 2
        flip = high + h - 2 * high * h
        return LAST - LAST * flip

    def piece(h, k):
        rank = ranks[h]
        p = k // PER_PARAM
        rest = k % PER_PARAM
        slot = (rest // SPLIT + slot_own) % 8
        chunk = slot // 2 + 4 * (slot % 2)
        z0 = (rest % SPLIT) * PIECE
        x0 = pl.multiple_of(chunk * ROWS, ROWS)
        own = grads.at[p, pl.ds(z0, PIECE), pl.ds(x0, ROWS), pl.ds(h * HALF, HALF)]

        @pl.when(rank == 0)
        def _():
            send_piece(own, h, k)

        @pl.when(rank > 0)
        def _():
            pltpu.make_async_copy(held.at[h, k], held.at[h, k], stream_recv.at[h, k]).wait()

        @pl.when((rank > 0) & (rank < LAST))
        def _():
            held[h, k] = (held[h, k].astype(F32) + own[...].astype(F32)).astype(BF16)
            send_piece(held.at[h, k], h, k)

        @pl.when(rank == LAST)
        def _():
            total = held[h, k].astype(F32) + own[...].astype(F32)
            r0 = pl.multiple_of(z0 * ROWS, PIECE * ROWS)
            turn[pl.ds(r0, PIECE * ROWS), :] = total.reshape(PIECE * ROWS, HALF)

            @pl.when(rest % SPLIT == SPLIT - 1)
            def _():
                for j in range(8):
                    g = 8 * j + slot
                    for i in range(2):
                        parts[p, g, :, i * HALF : (i + 1) * HALF] = turn[
                            pl.ds(2 * j + i, ROWS, stride=ROWS), :
                        ].astype(BF16)

                def to_owner(j, carry):
                    g = 8 * j + slot
                    d0 = pl.multiple_of(slab * ROWS, ROWS)

                    @pl.when(g != slab)
                    def _():
                        pltpu.make_async_remote_copy(
                            src_ref=parts.at[p, g], dst_ref=pencil.at[p, pl.ds(d0, ROWS), :],
                            send_sem=part_send, recv_sem=part_recv.at[p],
                            device_id={"shot": owner_of(h, g), "slab": g}, device_id_type=MESH,
                        ).start()

                    @pl.when(g == slab)
                    def _():
                        pltpu.make_async_copy(
                            parts.at[p, g], pencil.at[p, pl.ds(d0, ROWS), :], part_recv.at[p]
                        ).start()

                    return carry

                lax.fori_loop(0, 8, to_owner, 0)

    def build(t):
        p = t // (NZ // BUILD)
        first = (t % (NZ // BUILD)) * BUILD

        def rows(r, carry):
            lane = lax.broadcasted_iota(jnp.int32, (ROWS, BUILD), 1)
            sub = lax.broadcasted_iota(jnp.int32, (ROWS, BUILD), 0)
            three = widths[:, pl.ds(pl.multiple_of(first, BUILD), BUILD)]
            width_row = jnp.where(p == 0, three[0:1], jnp.where(p == 1, three[1:2], three[2:3]))
            width = jnp.sum(jnp.where(lane == sub + r * ROWS, width_row, 0.0), axis=1, keepdims=True)
            scale = -0.5 / (width * width)
            column = lax.broadcasted_iota(jnp.int32, (ROWS, NZ), 1)
            row = lax.broadcasted_iota(jnp.int32, (ROWS, NZ), 0) + (first + r * ROWS)
            offset = (column - row).astype(F32)
            bell = jnp.exp(offset * offset * scale)
            inverse = 1.0 / jnp.sum(bell, axis=1, keepdims=True)
            r0 = pl.multiple_of(first + r * ROWS, ROWS)
            matrix[p, pl.ds(r0, ROWS), :] = (bell * inverse).astype(BF16)
            return carry

        lax.fori_loop(0, BUILD // ROWS, rows, 0)

    def smooth(p):
        pltpu.make_async_copy(pencil.at[p], pencil.at[p], part_recv.at[p]).wait()

        def block(b, carry):
            which = (b + slab // ROWS) % (NZ // BLOCK)
            r0 = pl.multiple_of(which * BLOCK, BLOCK)
            value = jnp.dot(matrix[p, pl.ds(r0, BLOCK), :], pencil[p], preferred_element_type=F32)
            d0 = which * (BLOCK // ROWS)
            product[p, pl.ds(d0, BLOCK // ROWS)] = value.astype(BF16).reshape(BLOCK // ROWS, ROWS, 2 * HALF)

            def to_slab(i, inner):
                d = d0 + (i + slab) % (BLOCK // ROWS)
                here = (d == slab) & (chunk_own == shot)

                @pl.when(jnp.logical_not(here))
                def _():
                    pltpu.make_async_remote_copy(
                        src_ref=product.at[p, d], dst_ref=back.at[end_half, pair_own, p],
                        send_sem=back_send, recv_sem=back_recv,
                        device_id={"shot": chunk_own, "slab": d}, device_id_type=MESH,
                    ).start()

                @pl.when(here)
                def _():
                    pltpu.make_async_copy(
                        product.at[p, d], back.at[end_half, pair_own, p], back_recv
                    ).start()

                return inner

            lax.fori_loop(0, BLOCK // ROWS, to_slab, 0)
            return carry

        lax.fori_loop(0, NZ // BLOCK, block, 0)

    def at_step(t, carry):
        for h in range(2):
            k = t - SKEW * ranks[h]

            @pl.when((k >= 0) & (k < PIECES))
            def _():
                piece(h, k)

        @pl.when(is_end & (t < STEPS_BUILD))
        def _():
            build(t)

        after = t - SKEW * LAST - PER_PARAM - LAG

        @pl.when(is_end & (after >= 0) & (after % PER_PARAM == 0))
        def _():
            smooth(after // PER_PARAM)

        return carry

    lax.fori_loop(0, SKEW * LAST + PIECES + LAG + 1, at_step, 0)

    def waves(z, carry):
        angle = tilt[z]
        wave[0, z] = jnp.cos(angle)
        wave[1, z] = jnp.sin(angle)
        return carry

    lax.fori_loop(0, ROWS, waves, 0)

    pltpu.make_async_copy(back, back, back_recv).wait()

    for h in range(2):
        ys = slice(h * HALF, (h + 1) * HALF)
        for p in range(3):
            for j in range(8):
                for i in range(2):
                    x = 2 * j + i
                    flat[p, x * ROWS : (x + 1) * ROWS, :] = back[h, j, p, :, i * HALF : (i + 1) * HALF].astype(F32)

        def update(z, carry):
            new = [
                model[p, z, :, ys] - step[p] * flat[p, pl.ds(z, ROWS, stride=ROWS), :]
                for p in range(3)
            ]
            squared = new[0] * new[0]
            along = squared * (1.0 + 2.0 * new[1])
            normal = squared * (1.0 + 2.0 * new[2])
            cosine = wave[0, z, :, ys]
            sine = wave[1, z, :, ys]
            cc = cosine * cosine
            ss = sine * sine
            values = (along * cc + squared * ss, along * ss + squared * cc, (normal - squared) * (sine * cosine))
            for n in range(3):
                r0 = pl.multiple_of((z + 1) * ROWS, ROWS)
                rot[h, n, pl.ds(r0, ROWS), :] = values[n]
            return carry

        lax.fori_loop(0, ROWS, update, 0)
        for n in range(3):
            border[0, n, :, ys] = rot[h, n, pl.ds(ROWS, ROWS, stride=ROWS), :]
            border[1, n, :, ys] = rot[h, n, pl.ds(2 * ROWS - 1, ROWS, stride=ROWS), :]

    for s in range(2):
        for n in range(3):
            corner[s, 0, n : n + 1, :] = border[s, n, 0:1, :]
            corner[s, 1, n : n + 1, :] = border[s, n, ROWS - 1 : ROWS, :]

    moves = []
    for index, (dx, dz) in enumerate(
        ((0, 1), (0, -1), (1, 0), (-1, 0), (1, 1), (1, -1), (-1, 1), (-1, -1))
    ):
        xs = 1 if dx > 0 else 0
        zs = 1 if dz > 0 else 0
        if dx == 0:
            source = rot.at[:, :, pl.ds(ROWS * (ROWS if dz > 0 else 1), ROWS), :]
            target = rot.at[:, :, pl.ds(0 if dz > 0 else ROWS * (ROWS + 1), ROWS), :]
        elif dz == 0:
            source = border.at[xs]
            target = side.at[1 - xs, :, pl.ds(8, ROWS), :]
        else:
            source = corner.at[xs, zs]
            target = near.at[1 - xs, 1 - zs]
        copy = pltpu.make_async_remote_copy(
            src_ref=source, dst_ref=target, send_sem=halo_send.at[index], recv_sem=halo_recv.at[index],
            device_id={"shot": shot + dx, "slab": slab + dz}, device_id_type=MESH,
        )
        goes = (shot + dx >= 0) & (shot + dx < SHOTS) & (slab + dz >= 0) & (slab + dz < SLABS)
        comes = (shot - dx >= 0) & (shot - dx < SHOTS) & (slab - dz >= 0) & (slab - dz < SLABS)
        moves.append((copy, goes, comes, target, dx, dz))

    for copy, goes, comes, target, dx, dz in moves:
        @pl.when(goes)
        def _():
            copy.start()

        if dx != 0:
            @pl.when(jnp.logical_not(comes))
            def _():
                target[...] = jnp.zeros(target.shape, F32)

    for h in range(2):
        @pl.when(ranks[h] < LAST)
        def _():
            pltpu.make_async_copy(held.at[h], held.at[h], stream_send.at[h]).wait()

    @pl.when(is_end)
    def _():
        others = parts.at[:, pl.ds(0, SLABS - 1)]
        pltpu.make_async_copy(others, others, part_send).wait()

    @pl.when(is_end & (chunk_own == shot))
    def _():
        others = product.at[:, pl.ds(0, SLABS - 1)]
        pltpu.make_async_copy(others, others, back_send).wait()

    @pl.when(is_end & (chunk_own != shot))
    def _():
        pltpu.make_async_copy(product, product, back_send).wait()

    for copy, goes, comes, target, dx, dz in moves:
        @pl.when(comes)
        def _():
            copy.wait_recv()

    for s in range(2):
        for n in range(3):
            side[s, n, 7:8, :] = near[s, 0, n : n + 1, :]
            side[s, n, 8 + ROWS : 9 + ROWS, :] = near[s, 1, n : n + 1, :]
            edge[s, n] = (
                0.25 * (side[s, n, 7 : 7 + ROWS, :] + side[s, n, 9 : 9 + ROWS, :]) + 0.5 * side[s, n, 8 : 8 + ROWS, :]
            )

    def average(group, carry):
        x_at = lax.broadcasted_iota(jnp.int32, (ROWS, HALF), 0)
        z0 = pl.multiple_of(group * 8, 8)
        for n in range(3):
            for h in range(2):
                ys = slice(h * HALF, (h + 1) * HALF)
                low = edge[0, n, pl.ds(z0, 8), ys]
                high = edge[1, n, pl.ds(z0, 8), ys]
                for i in range(8):
                    three = [
                        rot[h, n, pl.ds(pl.multiple_of((z0 + i + j) * ROWS, ROWS), ROWS), :] for j in range(3)
                    ]
                    mean = 0.25 * (three[0] + three[2]) + 0.5 * three[1]
                    before = jnp.where(x_at == 0, low[i : i + 1], pltpu.roll(mean, 1, 0))
                    after = jnp.where(x_at == ROWS - 1, high[i : i + 1], pltpu.roll(mean, ROWS - 1, 0))
                    out[n, z0 + i, :, ys] = 0.25 * (before + after) + 0.5 * mean
        return carry

    lax.fori_loop(0, ROWS // 8, average, 0)

    for copy, goes, comes, target, dx, dz in moves:
        @pl.when(goes)
        def _():
            copy.wait_send()


def shards(partial_grads, model, tilt, widths, step_length):
    vmem = pl.BlockSpec(memory_space=pltpu.VMEM)
    wide = 2 * HALF
    return pl.pallas_call(
        kernel,
        out_shape=jax.ShapeDtypeStruct(model.shape, F32),
        in_specs=[vmem, vmem, vmem, vmem, pl.BlockSpec(memory_space=pltpu.SMEM)],
        out_specs=vmem,
        scratch_shapes=[
            pltpu.VMEM((2, PIECES, PIECE, ROWS, HALF), BF16),
            pltpu.VMEM((ROWS * ROWS, HALF), F32),
            pltpu.VMEM((3, SLABS, ROWS, wide), BF16),
            pltpu.VMEM((3, NZ, wide), BF16),
            pltpu.VMEM((3, NZ, NZ), BF16),
            pltpu.VMEM((3, SLABS, ROWS, wide), BF16),
            pltpu.VMEM((2, 8, 3, ROWS, wide), BF16),
            pltpu.VMEM((3, ROWS * ROWS, HALF), F32),
            pltpu.VMEM((2, ROWS, ROWS, wide), F32),
            pltpu.VMEM((2, 3, (ROWS + 2) * ROWS, HALF), F32),
            pltpu.VMEM((2, 3, ROWS, wide), F32),
            pltpu.VMEM((2, 2, 8, wide), F32),
            pltpu.VMEM((2, 3, 2 * ROWS, wide), F32),
            pltpu.VMEM((2, 2, 8, wide), F32),
            pltpu.VMEM((2, 3, ROWS, wide), F32),
            pltpu.SemaphoreType.DMA((2,)),
            pltpu.SemaphoreType.DMA((2, PIECES)),
            pltpu.SemaphoreType.DMA,
            pltpu.SemaphoreType.DMA((3,)),
            pltpu.SemaphoreType.DMA,
            pltpu.SemaphoreType.DMA,
            pltpu.SemaphoreType.DMA((8,)),
            pltpu.SemaphoreType.DMA((8,)),
        ],
        compiler_params=pltpu.CompilerParams(has_side_effects=True, vmem_limit_bytes=48 * 1024 * 1024),
    )(partial_grads[0], model, tilt, widths, step_length)


def solution(mesh):
    placed = (
        P("shot", None, "slab", None, None),
        P(None, "slab", "shot", None),
        P("slab", "shot", None),
        P(),
        P(),
    )
    return jax.shard_map(
        shards, mesh=mesh, in_specs=placed, out_specs=P(None, "slab", "shot", None), check_vma=False
    )
```

```python
import jax
import jax.numpy as jnp
from jax import lax
from jax.experimental import pallas as pl
from jax.experimental.pallas import tpu as pltpu
from jax.sharding import PartitionSpec as P

MESH = pl.DeviceIdType.MESH
F32 = jnp.float32
BF16 = jnp.bfloat16

SHOTS = 8
SLABS = 64
LAST = SHOTS - 1
ROWS = 16
HALF = 128
NZ = ROWS * SLABS
PIECE = 8
SPLIT = ROWS // PIECE
PER_PARAM = SHOTS * SPLIT
PIECES = 3 * PER_PARAM
SKEW = 4
LAG = 8
BLOCK = 256
UNROLL = 4
BUILD = 128
STEPS_BUILD = 3 * NZ // BUILD


def kernel(
    grads_hbm, model_hbm, tilt_hbm, widths_hbm, step_hbm, out,
    grads, model, tilt, widths, step, held, turn, parts, pencil, matrix, product, back, flat, wave, rot, border, corner, side, near, edge,
    load, stream_send, stream_recv, part_send, part_recv, back_send, back_recv, halo_send, halo_recv,
):
    shot = lax.axis_index("shot")
    slab = lax.axis_index("slab")
    upper = (slab // 8) % 2
    rank_0 = shot + upper * (LAST - 2 * shot)
    sign_0 = 1 - 2 * upper
    ranks = (rank_0, LAST - rank_0)
    signs = (sign_0, -sign_0)
    is_end = (rank_0 == 0) | (rank_0 == LAST)
    end_half = jnp.where(rank_0 == LAST, 0, 1)
    slot_own = slab % 8
    pair_own = slab // 8
    chunk_own = slot_own // 2 + 4 * (slot_own % 2)

    def owner_of(h, g):
        high = (g // 8) % 2
        flip = high + h - 2 * high * h
        return LAST - LAST * flip

    loads = [
        pltpu.make_async_copy(source, target, load.at[n])
        for n, (source, target) in enumerate(
            ((grads_hbm, grads), (widths_hbm, widths), (tilt_hbm, tilt), (model_hbm, model), (step_hbm, step))
        )
    ]
    for copy in loads:
        copy.start()
    barrier = pltpu.get_barrier_semaphore()

    @pl.when(shot > 0)
    def _():
        pl.semaphore_signal(barrier, inc=1, device_id={"shot": shot - 1, "slab": slab}, device_id_type=MESH)

    @pl.when(shot < LAST)
    def _():
        pl.semaphore_signal(barrier, inc=1, device_id={"shot": shot + 1, "slab": slab}, device_id_type=MESH)

    @pl.when(is_end)
    def _():
        def greet(i, carry):
            g = (slab + i) % SLABS
            pl.semaphore_signal(
                barrier, inc=1, device_id={"shot": owner_of(end_half, g), "slab": g}, device_id_type=MESH
            )
            return carry

        lax.fori_loop(1, SLABS, greet, 0)

    has = {"low": shot > 0, "high": shot < LAST}
    deep = {"low": slab > 0, "high": slab < SLABS - 1}
    corner[...] = jnp.zeros_like(corner)

    @pl.when(jnp.logical_not(deep["low"]))
    def _():
        rot[:, :, 0:ROWS] = jnp.zeros((2, 3, ROWS, HALF), F32)

    @pl.when(jnp.logical_not(deep["high"]))
    def _():
        rot[:, :, ROWS * (ROWS + 1) :] = jnp.zeros((2, 3, ROWS, HALF), F32)

    def send_piece(src, h, k):
        pltpu.make_async_remote_copy(
            src_ref=src, dst_ref=held.at[h, k], send_sem=stream_send.at[h], recv_sem=stream_recv.at[h, k],
            device_id={"shot": shot + signs[h], "slab": slab}, device_id_type=MESH,
        ).start()

    def piece(h, k):
        rank = ranks[h]
        p = k // PER_PARAM
        rest = k % PER_PARAM
        slot = (rest // SPLIT + slot_own) % 8
        chunk = slot // 2 + 4 * (slot % 2)
        z0 = (rest % SPLIT) * PIECE
        x0 = pl.multiple_of(chunk * ROWS, ROWS)
        where = (p, pl.ds(z0, PIECE), pl.ds(x0, ROWS), pl.ds(h * HALF, HALF))
        own = grads.at[where]

        @pl.when(rank == 0)
        def _():
            send_piece(grads_hbm.at[where], h, k)

        @pl.when(rank > 0)
        def _():
            pltpu.make_async_copy(held.at[h, k], held.at[h, k], stream_recv.at[h, k]).wait()

        @pl.when((rank > 0) & (rank < LAST))
        def _():
            held[h, k] = (held[h, k].astype(F32) + own[...].astype(F32)).astype(BF16)
            send_piece(held.at[h, k], h, k)

        @pl.when(rank == LAST)
        def _():
            total = held[h, k].astype(F32) + own[...].astype(F32)
            r0 = pl.multiple_of(z0 * ROWS, PIECE * ROWS)
            turn[pl.ds(r0, PIECE * ROWS), :] = total.reshape(PIECE * ROWS, HALF)

            @pl.when(rest % SPLIT == SPLIT - 1)
            def _():
                for j in range(8):
                    g = 8 * j + slot
                    for i in range(2):
                        parts[p, g, :, i * HALF : (i + 1) * HALF] = turn[
                            pl.ds(2 * j + i, ROWS, stride=ROWS), :
                        ].astype(BF16)

                def to_owner(j, carry):
                    g = 8 * j + slot
                    d0 = pl.multiple_of(slab * ROWS, ROWS)

                    @pl.when(g != slab)
                    def _():
                        pltpu.make_async_remote_copy(
                            src_ref=parts.at[p, g], dst_ref=pencil.at[p, pl.ds(d0, ROWS), :],
                            send_sem=part_send, recv_sem=part_recv.at[p],
                            device_id={"shot": owner_of(h, g), "slab": g}, device_id_type=MESH,
                        ).start()

                    @pl.when(g == slab)
                    def _():
                        pltpu.make_async_copy(
                            parts.at[p, g], pencil.at[p, pl.ds(d0, ROWS), :], part_recv.at[p]
                        ).start()

                    return carry

                lax.fori_loop(0, 8, to_owner, 0)

    def build(t):
        p = t // (NZ // BUILD)
        first = (t % (NZ // BUILD)) * BUILD

        def rows(r, carry):
            lane = lax.broadcasted_iota(jnp.int32, (ROWS, BUILD), 1)
            sub = lax.broadcasted_iota(jnp.int32, (ROWS, BUILD), 0)
            three = widths[:, pl.ds(pl.multiple_of(first, BUILD), BUILD)]
            width_row = jnp.where(p == 0, three[0:1], jnp.where(p == 1, three[1:2], three[2:3]))
            width = jnp.sum(jnp.where(lane == sub + r * ROWS, width_row, 0.0), axis=1, keepdims=True)
            scale = -0.5 / (width * width)
            column = lax.broadcasted_iota(jnp.int32, (ROWS, NZ), 1)
            row = lax.broadcasted_iota(jnp.int32, (ROWS, NZ), 0) + (first + r * ROWS)
            offset = (column - row).astype(F32)
            bell = jnp.exp(offset * offset * scale)
            inverse = 1.0 / jnp.sum(bell, axis=1, keepdims=True)
            r0 = pl.multiple_of(first + r * ROWS, ROWS)
            matrix[p, pl.ds(r0, ROWS), :] = (bell * inverse).astype(BF16)
            return carry

        lax.fori_loop(0, BUILD // ROWS, rows, 0, unroll=UNROLL)

    def smooth(p):
        pltpu.make_async_copy(pencil.at[p], pencil.at[p], part_recv.at[p]).wait()

        def block(b, carry):
            which = (b + slab // ROWS) % (NZ // BLOCK)
            r0 = pl.multiple_of(which * BLOCK, BLOCK)
            value = jnp.dot(matrix[p, pl.ds(r0, BLOCK), :], pencil[p], preferred_element_type=F32)
            d0 = which * (BLOCK // ROWS)
            product[p, pl.ds(d0, BLOCK // ROWS)] = value.astype(BF16).reshape(BLOCK // ROWS, ROWS, 2 * HALF)

            def to_slab(i, inner):
                d = d0 + (i + slab) % (BLOCK // ROWS)
                here = (d == slab) & (chunk_own == shot)

                @pl.when(jnp.logical_not(here))
                def _():
                    pltpu.make_async_remote_copy(
                        src_ref=product.at[p, d], dst_ref=back.at[end_half, pair_own, p],
                        send_sem=back_send, recv_sem=back_recv,
                        device_id={"shot": chunk_own, "slab": d}, device_id_type=MESH,
                    ).start()

                @pl.when(here)
                def _():
                    pltpu.make_async_copy(
                        product.at[p, d], back.at[end_half, pair_own, p], back_recv
                    ).start()

                return inner

            lax.fori_loop(0, BLOCK // ROWS, to_slab, 0)
            return carry

        lax.fori_loop(0, NZ // BLOCK, block, 0)

    pl.semaphore_wait(barrier, jnp.where(is_end, SLABS, 2))
    loads[0].wait()
    loads[1].wait()

    def at_step(t, carry):
        for h in range(2):
            k = t - SKEW * ranks[h]

            @pl.when((k >= 0) & (k < PIECES))
            def _():
                piece(h, k)

        @pl.when(is_end & (t < STEPS_BUILD))
        def _():
            build(t)

        after = t - SKEW * LAST - PER_PARAM - LAG

        @pl.when(is_end & (after >= 0) & (after % PER_PARAM == 0))
        def _():
            smooth(after // PER_PARAM)

        return carry

    lax.fori_loop(0, SKEW * LAST + PIECES + LAG + 1, at_step, 0)

    for copy in loads[2:]:
        copy.wait()

    def waves(z, carry):
        angle = tilt[z]
        wave[0, z] = jnp.cos(angle)
        wave[1, z] = jnp.sin(angle)
        return carry

    lax.fori_loop(0, ROWS, waves, 0)

    pltpu.make_async_copy(back, back, back_recv).wait()

    for h in range(2):
        ys = slice(h * HALF, (h + 1) * HALF)
        for p in range(3):
            for j in range(8):
                for i in range(2):
                    x = 2 * j + i
                    flat[p, x * ROWS : (x + 1) * ROWS, :] = back[h, j, p, :, i * HALF : (i + 1) * HALF].astype(F32)

        def update(z, carry):
            new = [
                model[p, z, :, ys] - step[p] * flat[p, pl.ds(z, ROWS, stride=ROWS), :]
                for p in range(3)
            ]
            squared = new[0] * new[0]
            along = squared * (1.0 + 2.0 * new[1])
            normal = squared * (1.0 + 2.0 * new[2])
            cosine = wave[0, z, :, ys]
            sine = wave[1, z, :, ys]
            cc = cosine * cosine
            ss = sine * sine
            values = (along * cc + squared * ss, along * ss + squared * cc, (normal - squared) * (sine * cosine))
            for n in range(3):
                r0 = pl.multiple_of((z + 1) * ROWS, ROWS)
                rot[h, n, pl.ds(r0, ROWS), :] = values[n]
            return carry

        lax.fori_loop(0, ROWS, update, 0)
        for n in range(3):
            border[0, n, :, ys] = rot[h, n, pl.ds(ROWS, ROWS, stride=ROWS), :]
            border[1, n, :, ys] = rot[h, n, pl.ds(2 * ROWS - 1, ROWS, stride=ROWS), :]

    for s in range(2):
        for n in range(3):
            corner[s, 0, n : n + 1, :] = border[s, n, 0:1, :]
            corner[s, 1, n : n + 1, :] = border[s, n, ROWS - 1 : ROWS, :]

    moves = []
    for index, (dx, dz) in enumerate(
        ((0, 1), (0, -1), (1, 0), (-1, 0), (1, 1), (1, -1), (-1, 1), (-1, -1))
    ):
        xs = 1 if dx > 0 else 0
        zs = 1 if dz > 0 else 0
        if dx == 0:
            source = rot.at[:, :, pl.ds(ROWS * (ROWS if dz > 0 else 1), ROWS), :]
            target = rot.at[:, :, pl.ds(0 if dz > 0 else ROWS * (ROWS + 1), ROWS), :]
        elif dz == 0:
            source = border.at[xs]
            target = side.at[1 - xs, :, pl.ds(8, ROWS), :]
        else:
            source = corner.at[xs, zs]
            target = near.at[1 - xs, 1 - zs]
        copy = pltpu.make_async_remote_copy(
            src_ref=source, dst_ref=target, send_sem=halo_send.at[index], recv_sem=halo_recv.at[index],
            device_id={"shot": shot + dx, "slab": slab + dz}, device_id_type=MESH,
        )
        goes = (shot + dx >= 0) & (shot + dx < SHOTS) & (slab + dz >= 0) & (slab + dz < SLABS)
        comes = (shot - dx >= 0) & (shot - dx < SHOTS) & (slab - dz >= 0) & (slab - dz < SLABS)
        moves.append((copy, goes, comes, target, dx, dz))

    for copy, goes, comes, target, dx, dz in moves:
        @pl.when(goes)
        def _():
            copy.start()

        if dx != 0:
            @pl.when(jnp.logical_not(comes))
            def _():
                target[...] = jnp.zeros(target.shape, F32)

    for h in range(2):
        @pl.when(ranks[h] < LAST)
        def _():
            pltpu.make_async_copy(held.at[h], held.at[h], stream_send.at[h]).wait()

    @pl.when(is_end)
    def _():
        others = parts.at[:, pl.ds(0, SLABS - 1)]
        pltpu.make_async_copy(others, others, part_send).wait()

    @pl.when(is_end & (chunk_own == shot))
    def _():
        others = product.at[:, pl.ds(0, SLABS - 1)]
        pltpu.make_async_copy(others, others, back_send).wait()

    @pl.when(is_end & (chunk_own != shot))
    def _():
        pltpu.make_async_copy(product, product, back_send).wait()

    for copy, goes, comes, target, dx, dz in moves:
        @pl.when(comes)
        def _():
            copy.wait_recv()

    for s in range(2):
        for n in range(3):
            side[s, n, 7:8, :] = near[s, 0, n : n + 1, :]
            side[s, n, 8 + ROWS : 9 + ROWS, :] = near[s, 1, n : n + 1, :]
            edge[s, n] = (
                0.25 * (side[s, n, 7 : 7 + ROWS, :] + side[s, n, 9 : 9 + ROWS, :]) + 0.5 * side[s, n, 8 : 8 + ROWS, :]
            )

    def average(group, carry):
        x_at = lax.broadcasted_iota(jnp.int32, (ROWS, HALF), 0)
        z0 = pl.multiple_of(group * 8, 8)
        for n in range(3):
            for h in range(2):
                ys = slice(h * HALF, (h + 1) * HALF)
                low = edge[0, n, pl.ds(z0, 8), ys]
                high = edge[1, n, pl.ds(z0, 8), ys]
                for i in range(8):
                    three = [
                        rot[h, n, pl.ds(pl.multiple_of((z0 + i + j) * ROWS, ROWS), ROWS), :] for j in range(3)
                    ]
                    mean = 0.25 * (three[0] + three[2]) + 0.5 * three[1]
                    before = jnp.where(x_at == 0, low[i : i + 1], pltpu.roll(mean, 1, 0))
                    after = jnp.where(x_at == ROWS - 1, high[i : i + 1], pltpu.roll(mean, ROWS - 1, 0))
                    out[n, z0 + i, :, ys] = 0.25 * (before + after) + 0.5 * mean
        return carry

    lax.fori_loop(0, ROWS // 8, average, 0)

    for copy, goes, comes, target, dx, dz in moves:
        @pl.when(goes)
        def _():
            copy.wait_send()


def shards(partial_grads, model, tilt, widths, step_length):
    vmem = pl.BlockSpec(memory_space=pltpu.VMEM)
    hbm = pl.BlockSpec(memory_space=pl.ANY)
    wide = 2 * HALF
    return pl.pallas_call(
        kernel,
        out_shape=jax.ShapeDtypeStruct(model.shape, F32),
        in_specs=[hbm] * 5,
        out_specs=vmem,
        scratch_shapes=[
            pltpu.VMEM(partial_grads.shape[1:], BF16),
            pltpu.VMEM(model.shape, F32),
            pltpu.VMEM(tilt.shape, F32),
            pltpu.VMEM(widths.shape, F32),
            pltpu.SMEM(step_length.shape, F32),
            pltpu.VMEM((2, PIECES, PIECE, ROWS, HALF), BF16),
            pltpu.VMEM((ROWS * ROWS, HALF), F32),
            pltpu.VMEM((3, SLABS, ROWS, wide), BF16),
            pltpu.VMEM((3, NZ, wide), BF16),
            pltpu.VMEM((3, NZ, NZ), BF16),
            pltpu.VMEM((3, SLABS, ROWS, wide), BF16),
            pltpu.VMEM((2, 8, 3, ROWS, wide), BF16),
            pltpu.VMEM((3, ROWS * ROWS, HALF), F32),
            pltpu.VMEM((2, ROWS, ROWS, wide), F32),
            pltpu.VMEM((2, 3, (ROWS + 2) * ROWS, HALF), F32),
            pltpu.VMEM((2, 3, ROWS, wide), F32),
            pltpu.VMEM((2, 2, 8, wide), F32),
            pltpu.VMEM((2, 3, 2 * ROWS, wide), F32),
            pltpu.VMEM((2, 2, 8, wide), F32),
            pltpu.VMEM((2, 3, ROWS, wide), F32),
            pltpu.SemaphoreType.DMA((5,)),
            pltpu.SemaphoreType.DMA((2,)),
            pltpu.SemaphoreType.DMA((2, PIECES)),
            pltpu.SemaphoreType.DMA,
            pltpu.SemaphoreType.DMA((3,)),
            pltpu.SemaphoreType.DMA,
            pltpu.SemaphoreType.DMA,
            pltpu.SemaphoreType.DMA((8,)),
            pltpu.SemaphoreType.DMA((8,)),
        ],
        compiler_params=pltpu.CompilerParams(
            collective_id=0, has_side_effects=True, vmem_limit_bytes=60 * 1024 * 1024
        ),
    )(partial_grads[0], model, tilt, widths, step_length)


def solution(mesh):
    placed = (
        P("shot", None, "slab", None, None),
        P(None, "slab", "shot", None),
        P("slab", "shot", None),
        P(),
        P(),
    )
    return jax.shard_map(
        shards, mesh=mesh, in_specs=placed, out_specs=P(None, "slab", "shot", None), check_vma=False
    )
```

```python
import jax
import jax.numpy as jnp
from jax import lax
from jax.experimental import pallas as pl
from jax.experimental.pallas import tpu as pltpu
from jax.sharding import PartitionSpec as P

MESH = pl.DeviceIdType.MESH
F32 = jnp.float32
BF16 = jnp.bfloat16

SHOTS = 8
SLABS = 64
LAST = SHOTS - 1
ROWS = 16
HALF = 128
NZ = ROWS * SLABS
PIECE = 8
SPLIT = ROWS // PIECE
PER_PARAM = SHOTS * SPLIT
PIECES = 3 * PER_PARAM
SKEW = 11
LAG = 16
BLOCK = 256
UNROLL = 4
FILL = (SKEW * LAST) // 2
GREET_STEPS = (SLABS - 1) // 3
BUILD = 128
STEPS_BUILD = 3 * NZ // BUILD


def chunk_of(slot):
    return slot // 2 + (slot % 2) * (LAST - 2 * (slot // 2))


def owner_slab(pair, slot):
    return (pair % 4) * 16 + (pair // 4) * 8 + ((pair + slot) % 4) * 2 + slot // 4


def kernel(
    grads_hbm, model_hbm, tilt_hbm, widths_hbm, step_hbm, out,
    grads, model, tilt, widths, step, held, turn, parts, pencil, matrix, product, back, flat, wave, rot, border, corner, side, near, edge,
    there, load, stream_send, stream_recv, part_send, part_recv, back_send, back_recv, halo_send, halo_recv,
):
    shot = lax.axis_index("shot")
    slab = lax.axis_index("slab")
    upper = (slab // 8) % 2
    rank_0 = shot + upper * (LAST - 2 * shot)
    sign_0 = 1 - 2 * upper
    ranks = (rank_0, LAST - rank_0)
    signs = (sign_0, -sign_0)
    is_end = (rank_0 == 0) | (rank_0 == LAST)
    end_half = jnp.where(rank_0 == LAST, 0, 1)
    slab_x, slab_y = slab // 16, (slab // 2) % 4
    slot_own = (slab_y + 4 - slab_x) % 4 + 4 * (slab % 2)
    pair_own = slab_x + 4 * upper
    chunk_own = chunk_of(slot_own)

    def owner_of(h, g):
        high = (g // 8) % 2
        flip = high + h - 2 * high * h
        return LAST - LAST * flip

    loads = [
        pltpu.make_async_copy(source, target, load.at[n])
        for n, (source, target) in enumerate(
            ((grads_hbm, grads), (widths_hbm, widths), (tilt_hbm, tilt), (model_hbm, model), (step_hbm, step))
        )
    ]
    barrier = pltpu.get_barrier_semaphore()

    for to in (-1, 1):
        @pl.when((shot + to >= 0) & (shot + to < SHOTS) & (rank_0 + sign_0 * to > 0) & (rank_0 + sign_0 * to < LAST))
        def _():
            pl.semaphore_signal(barrier, inc=1, device_id={"shot": shot + to, "slab": slab}, device_id_type=MESH)

    def greet(i, carry):
        g = (slab + i) % SLABS
        pl.semaphore_signal(
            barrier, inc=1, device_id={"shot": owner_of(end_half, g), "slab": g}, device_id_type=MESH
        )
        return carry

    for copy in loads:
        copy.start()

    has = {"low": shot > 0, "high": shot < LAST}
    deep = {"low": slab > 0, "high": slab < SLABS - 1}
    corner[...] = jnp.zeros_like(corner)

    @pl.when(jnp.logical_not(deep["low"]))
    def _():
        rot[:, :, 0:ROWS] = jnp.zeros((2, 3, ROWS, HALF), F32)

    @pl.when(jnp.logical_not(deep["high"]))
    def _():
        rot[:, :, ROWS * (ROWS + 1) :] = jnp.zeros((2, 3, ROWS, HALF), F32)

    def send_piece(src, h, k):
        pltpu.make_async_remote_copy(
            src_ref=src, dst_ref=held.at[h, k], send_sem=stream_send.at[h], recv_sem=stream_recv.at[h, k],
            device_id={"shot": shot + signs[h], "slab": slab}, device_id_type=MESH,
        ).start()

    def piece(h, k, starts):
        rank = ranks[h]
        p = k // PER_PARAM
        rest = k % PER_PARAM
        slot = rest // SPLIT
        chunk = chunk_of(slot)
        z0 = (rest % SPLIT) * PIECE
        x0 = pl.multiple_of(chunk * ROWS, ROWS)
        where = (p, pl.ds(z0, PIECE), pl.ds(x0, ROWS), pl.ds(h * HALF, HALF))
        own = grads.at[where]

        if starts:
            send_piece(grads_hbm.at[where], h, k)
            return
        pltpu.make_async_copy(held.at[h, k], held.at[h, k], stream_recv.at[h, k]).wait()

        @pl.when(rank < LAST)
        def _():
            held[h, k] = (held[h, k].astype(F32) + own[...].astype(F32)).astype(BF16)
            send_piece(held.at[h, k], h, k)

        @pl.when(rank == LAST)
        def _():
            total = held[h, k].astype(F32) + own[...].astype(F32)
            r0 = pl.multiple_of(z0 * ROWS, PIECE * ROWS)
            turn[pl.ds(r0, PIECE * ROWS), :] = total.reshape(PIECE * ROWS, HALF)

            @pl.when(rest % SPLIT == SPLIT - 1)
            def _():
                for j in range(8):
                    g = owner_slab(j, slot)
                    for i in range(2):
                        parts[p, g, :, i * HALF : (i + 1) * HALF] = turn[
                            pl.ds(2 * j + i, ROWS, stride=ROWS), :
                        ].astype(BF16)

                def to_owner(i, carry):
                    g = owner_slab((i + slab) % 8, slot)
                    d0 = pl.multiple_of(slab * ROWS, ROWS)

                    @pl.when(g != slab)
                    def _():
                        pltpu.make_async_remote_copy(
                            src_ref=parts.at[p, g], dst_ref=pencil.at[p, pl.ds(d0, ROWS), :],
                            send_sem=part_send, recv_sem=part_recv.at[p],
                            device_id={"shot": owner_of(h, g), "slab": g}, device_id_type=MESH,
                        ).start()

                    @pl.when(g == slab)
                    def _():
                        pltpu.make_async_copy(
                            parts.at[p, g], pencil.at[p, pl.ds(d0, ROWS), :], part_recv.at[p]
                        ).start()

                    return carry

                lax.fori_loop(0, 8, to_owner, 0)

    def build(t):
        p = t // (NZ // BUILD)
        first = (t % (NZ // BUILD)) * BUILD

        def rows(r, carry):
            lane = lax.broadcasted_iota(jnp.int32, (ROWS, BUILD), 1)
            sub = lax.broadcasted_iota(jnp.int32, (ROWS, BUILD), 0)
            three = widths[:, pl.ds(pl.multiple_of(first, BUILD), BUILD)]
            width_row = jnp.where(p == 0, three[0:1], jnp.where(p == 1, three[1:2], three[2:3]))
            width = jnp.sum(jnp.where(lane == sub + r * ROWS, width_row, 0.0), axis=1, keepdims=True)
            scale = -0.5 / (width * width)
            column = lax.broadcasted_iota(jnp.int32, (ROWS, NZ), 1)
            row = lax.broadcasted_iota(jnp.int32, (ROWS, NZ), 0) + (first + r * ROWS)
            offset = (column - row).astype(F32)
            bell = jnp.exp(offset * offset * scale)
            inverse = 1.0 / jnp.sum(bell, axis=1, keepdims=True)
            r0 = pl.multiple_of(first + r * ROWS, ROWS)
            matrix[p, pl.ds(r0, ROWS), :] = (bell * inverse).astype(BF16)
            return carry

        lax.fori_loop(0, BUILD // ROWS, rows, 0, unroll=UNROLL)

    def smooth(p):
        pltpu.make_async_copy(pencil.at[p], pencil.at[p], part_recv.at[p]).wait()

        def block(b, carry):
            which = (b + slab // ROWS) % (NZ // BLOCK)
            r0 = pl.multiple_of(which * BLOCK, BLOCK)
            value = jnp.dot(matrix[p, pl.ds(r0, BLOCK), :], pencil[p], preferred_element_type=F32)
            d0 = which * (BLOCK // ROWS)
            product[p, pl.ds(d0, BLOCK // ROWS)] = value.astype(BF16).reshape(BLOCK // ROWS, ROWS, 2 * HALF)

            def to_slab(i, inner):
                d = d0 + (i + slab) % (BLOCK // ROWS)
                here = (d == slab) & (chunk_own == shot)

                @pl.when(jnp.logical_not(here))
                def _():
                    pltpu.make_async_remote_copy(
                        src_ref=product.at[p, d], dst_ref=back.at[end_half, pair_own, p],
                        send_sem=back_send, recv_sem=back_recv,
                        device_id={"shot": chunk_own, "slab": d}, device_id_type=MESH,
                    ).start()

                @pl.when(here)
                def _():
                    pltpu.make_async_copy(
                        product.at[p, d], back.at[end_half, pair_own, p], back_recv
                    ).start()

                return inner

            lax.fori_loop(0, BLOCK // ROWS, to_slab, 0)
            return carry

        lax.fori_loop(0, NZ // BLOCK, block, 0)

    @pl.when(jnp.logical_not(is_end))
    def _():
        pl.semaphore_wait(barrier, 2)

    for to in (-1, 1):
        @pl.when((shot + to >= 0) & (shot + to < SHOTS) & ((rank_0 + sign_0 * to == 0) | (rank_0 + sign_0 * to == LAST)))
        def _():
            pl.semaphore_signal(there, inc=1, device_id={"shot": shot + to, "slab": slab}, device_id_type=MESH)

    @pl.when(is_end)
    def _():
        pl.semaphore_wait(there, 1)

    def at_step(t, carry):
        for h in range(2):
            rank = ranks[h]
            k = t - (SKEW * rank) // 2

            @pl.when((rank == 0) & (t < PIECES // 2))
            def _():
                piece(h, 2 * t, True)
                piece(h, 2 * t + 1, True)

            if h == 0:
                @pl.when(t == 0)
                def _():
                    loads[0].wait()
                    loads[1].wait()

            @pl.when((rank > 0) & (k >= 0) & (k < PIECES))
            def _():
                piece(h, k, False)

        @pl.when(is_end & (t < GREET_STEPS))
        def _():
            lax.fori_loop(1 + 3 * t, 4 + 3 * t, greet, 0)

        @pl.when(is_end & (t < STEPS_BUILD))
        def _():
            build(t)

        @pl.when(is_end & (t == FILL - 1))
        def _():
            pl.semaphore_wait(barrier, SLABS - 1)

        after = t - FILL - SPLIT * (slot_own + 1) - LAG

        @pl.when(is_end & (after >= 0) & (after % PER_PARAM == 0) & (after < PIECES))
        def _():
            smooth(after // PER_PARAM)

        return carry

    lax.fori_loop(0, FILL + PIECES + LAG + 1, at_step, 0)

    for copy in loads[2:]:
        copy.wait()

    def waves(z, carry):
        angle = tilt[z]
        wave[0, z] = jnp.cos(angle)
        wave[1, z] = jnp.sin(angle)
        return carry

    lax.fori_loop(0, ROWS, waves, 0)

    pltpu.make_async_copy(back, back, back_recv).wait()

    for h in range(2):
        ys = slice(h * HALF, (h + 1) * HALF)
        for p in range(3):
            for j in range(8):
                for i in range(2):
                    x = 2 * j + i
                    flat[p, x * ROWS : (x + 1) * ROWS, :] = back[h, j, p, :, i * HALF : (i + 1) * HALF].astype(F32)

        def update(z, carry):
            new = [
                model[p, z, :, ys] - step[p] * flat[p, pl.ds(z, ROWS, stride=ROWS), :]
                for p in range(3)
            ]
            squared = new[0] * new[0]
            along = squared * (1.0 + 2.0 * new[1])
            normal = squared * (1.0 + 2.0 * new[2])
            cosine = wave[0, z, :, ys]
            sine = wave[1, z, :, ys]
            cc = cosine * cosine
            ss = sine * sine
            values = (along * cc + squared * ss, along * ss + squared * cc, (normal - squared) * (sine * cosine))
            for n in range(3):
                r0 = pl.multiple_of((z + 1) * ROWS, ROWS)
                rot[h, n, pl.ds(r0, ROWS), :] = values[n]
            return carry

        lax.fori_loop(0, ROWS, update, 0)
        for n in range(3):
            border[0, n, :, ys] = rot[h, n, pl.ds(ROWS, ROWS, stride=ROWS), :]
            border[1, n, :, ys] = rot[h, n, pl.ds(2 * ROWS - 1, ROWS, stride=ROWS), :]

    for s in range(2):
        for n in range(3):
            corner[s, 0, n : n + 1, :] = border[s, n, 0:1, :]
            corner[s, 1, n : n + 1, :] = border[s, n, ROWS - 1 : ROWS, :]

    moves = []
    for index, (dx, dz) in enumerate(
        ((0, 1), (0, -1), (1, 0), (-1, 0), (1, 1), (1, -1), (-1, 1), (-1, -1))
    ):
        xs = 1 if dx > 0 else 0
        zs = 1 if dz > 0 else 0
        if dx == 0:
            source = rot.at[:, :, pl.ds(ROWS * (ROWS if dz > 0 else 1), ROWS), :]
            target = rot.at[:, :, pl.ds(0 if dz > 0 else ROWS * (ROWS + 1), ROWS), :]
        elif dz == 0:
            source = border.at[xs]
            target = side.at[1 - xs, :, pl.ds(8, ROWS), :]
        else:
            source = corner.at[xs, zs]
            target = near.at[1 - xs, 1 - zs]
        copy = pltpu.make_async_remote_copy(
            src_ref=source, dst_ref=target, send_sem=halo_send.at[index], recv_sem=halo_recv.at[index],
            device_id={"shot": shot + dx, "slab": slab + dz}, device_id_type=MESH,
        )
        goes = (shot + dx >= 0) & (shot + dx < SHOTS) & (slab + dz >= 0) & (slab + dz < SLABS)
        comes = (shot - dx >= 0) & (shot - dx < SHOTS) & (slab - dz >= 0) & (slab - dz < SLABS)
        moves.append((copy, goes, comes, target, dx, dz))

    for copy, goes, comes, target, dx, dz in moves:
        @pl.when(goes)
        def _():
            copy.start()

        if dx != 0:
            @pl.when(jnp.logical_not(comes))
            def _():
                target[...] = jnp.zeros(target.shape, F32)

    for h in range(2):
        @pl.when(ranks[h] < LAST)
        def _():
            pltpu.make_async_copy(held.at[h], held.at[h], stream_send.at[h]).wait()

    @pl.when(is_end)
    def _():
        others = parts.at[:, pl.ds(0, SLABS - 1)]
        pltpu.make_async_copy(others, others, part_send).wait()

    @pl.when(is_end & (chunk_own == shot))
    def _():
        others = product.at[:, pl.ds(0, SLABS - 1)]
        pltpu.make_async_copy(others, others, back_send).wait()

    @pl.when(is_end & (chunk_own != shot))
    def _():
        pltpu.make_async_copy(product, product, back_send).wait()

    for copy, goes, comes, target, dx, dz in moves:
        @pl.when(comes)
        def _():
            copy.wait_recv()

    for s in range(2):
        for n in range(3):
            side[s, n, 7:8, :] = near[s, 0, n : n + 1, :]
            side[s, n, 8 + ROWS : 9 + ROWS, :] = near[s, 1, n : n + 1, :]
            edge[s, n] = (
                0.25 * (side[s, n, 7 : 7 + ROWS, :] + side[s, n, 9 : 9 + ROWS, :]) + 0.5 * side[s, n, 8 : 8 + ROWS, :]
            )

    def average(group, carry):
        x_at = lax.broadcasted_iota(jnp.int32, (ROWS, HALF), 0)
        z0 = pl.multiple_of(group * 8, 8)
        for n in range(3):
            for h in range(2):
                ys = slice(h * HALF, (h + 1) * HALF)
                low = edge[0, n, pl.ds(z0, 8), ys]
                high = edge[1, n, pl.ds(z0, 8), ys]
                for i in range(8):
                    three = [
                        rot[h, n, pl.ds(pl.multiple_of((z0 + i + j) * ROWS, ROWS), ROWS), :] for j in range(3)
                    ]
                    mean = 0.25 * (three[0] + three[2]) + 0.5 * three[1]
                    before = jnp.where(x_at == 0, low[i : i + 1], pltpu.roll(mean, 1, 0))
                    after = jnp.where(x_at == ROWS - 1, high[i : i + 1], pltpu.roll(mean, ROWS - 1, 0))
                    out[n, z0 + i, :, ys] = 0.25 * (before + after) + 0.5 * mean
        return carry

    lax.fori_loop(0, ROWS // 8, average, 0)

    for copy, goes, comes, target, dx, dz in moves:
        @pl.when(goes)
        def _():
            copy.wait_send()


def shards(partial_grads, model, tilt, widths, step_length):
    vmem = pl.BlockSpec(memory_space=pltpu.VMEM)
    hbm = pl.BlockSpec(memory_space=pl.ANY)
    wide = 2 * HALF
    return pl.pallas_call(
        kernel,
        out_shape=jax.ShapeDtypeStruct(model.shape, F32),
        in_specs=[hbm] * 5,
        out_specs=vmem,
        scratch_shapes=[
            pltpu.VMEM(partial_grads.shape[1:], BF16),
            pltpu.VMEM(model.shape, F32),
            pltpu.VMEM(tilt.shape, F32),
            pltpu.VMEM(widths.shape, F32),
            pltpu.SMEM(step_length.shape, F32),
            pltpu.VMEM((2, PIECES, PIECE, ROWS, HALF), BF16),
            pltpu.VMEM((ROWS * ROWS, HALF), F32),
            pltpu.VMEM((3, SLABS, ROWS, wide), BF16),
            pltpu.VMEM((3, NZ, wide), BF16),
            pltpu.VMEM((3, NZ, NZ), BF16),
            pltpu.VMEM((3, SLABS, ROWS, wide), BF16),
            pltpu.VMEM((2, 8, 3, ROWS, wide), BF16),
            pltpu.VMEM((3, ROWS * ROWS, HALF), F32),
            pltpu.VMEM((2, ROWS, ROWS, wide), F32),
            pltpu.VMEM((2, 3, (ROWS + 2) * ROWS, HALF), F32),
            pltpu.VMEM((2, 3, ROWS, wide), F32),
            pltpu.VMEM((2, 2, 8, wide), F32),
            pltpu.VMEM((2, 3, 2 * ROWS, wide), F32),
            pltpu.VMEM((2, 2, 8, wide), F32),
            pltpu.VMEM((2, 3, ROWS, wide), F32),
            pltpu.SemaphoreType.REGULAR,
            pltpu.SemaphoreType.DMA((5,)),
            pltpu.SemaphoreType.DMA((2,)),
            pltpu.SemaphoreType.DMA((2, PIECES)),
            pltpu.SemaphoreType.DMA,
            pltpu.SemaphoreType.DMA((3,)),
            pltpu.SemaphoreType.DMA,
            pltpu.SemaphoreType.DMA,
            pltpu.SemaphoreType.DMA((8,)),
            pltpu.SemaphoreType.DMA((8,)),
        ],
        compiler_params=pltpu.CompilerParams(
            collective_id=0, has_side_effects=True, vmem_limit_bytes=60 * 1024 * 1024
        ),
    )(partial_grads[0], model, tilt, widths, step_length)


def solution(mesh):
    placed = (
        P("shot", None, "slab", None, None),
        P(None, "slab", "shot", None),
        P("slab", "shot", None),
        P(),
        P(),
    )
    return jax.shard_map(
        shards, mesh=mesh, in_specs=placed, out_specs=P(None, "slab", "shot", None), check_vma=False
    )
```

```python
import jax
import jax.numpy as jnp
from jax import lax
from jax.experimental import pallas as pl
from jax.experimental.pallas import tpu as pltpu
from jax.sharding import PartitionSpec as P

MESH = pl.DeviceIdType.MESH
F32 = jnp.float32
BF16 = jnp.bfloat16

SHOTS = 8
SLABS = 64
LAST = SHOTS - 1
ROWS = 16
HALF = 128
QUAD = 4
QUADS = ROWS // QUAD
NZ = ROWS * SLABS
PER_PARAM = 2 * SHOTS
PIECES = 3 * PER_PARAM
BLOCK = 256
BUILD = 128
UNROLL = 4


def chunk_of(slot):
    return slot // 2 + (slot % 2) * (LAST - 2 * (slot // 2))


def kernel(
    grads_hbm, model_hbm, tilt_hbm, widths_hbm, step_hbm, out,
    mine, model, tilt, widths, step, held,
    turn, parts, pencil, matrix, product, back, flat, wave, rot, border, corner, side, near, edge,
    there, load, swap_send, swap_recv, stream_send, stream_recv, part_send, part_recv, back_send, back_recv,
    halo_send, halo_recv,
):
    shot = lax.axis_index("shot")
    slab = lax.axis_index("slab")
    core = slab % 2
    upper = (slab // 8) % 2
    slab_x, slab_y = slab // 16, (slab // 2) % 4
    other = slab + 1 - 2 * core
    turned = upper + core - 2 * upper * core
    rank = shot + turned * (LAST - 2 * shot)
    sign = 1 - 2 * turned
    is_first = rank == 0
    is_last = rank == LAST
    is_middle = (rank > 0) & (rank < LAST)
    y0 = pl.multiple_of(core * HALF, HALF)
    y0_other = pl.multiple_of((1 - core) * HALF, HALF)

    slot_own = (slab_y + 4 - slab_x) % 4 + 4 * ((upper + slab_x) % 2)
    chunk_own = chunk_of(slot_own)
    half_own = 1 - core

    def plane_of(h, high):
        flip = high + h - 2 * high * h
        return LAST - LAST * flip

    barrier = pltpu.get_barrier_semaphore()

    @pl.when(rank > 0)
    def _():
        pl.semaphore_signal(barrier, inc=1, device_id={"shot": shot - sign, "slab": slab}, device_id_type=MESH)
        pl.semaphore_signal(barrier, inc=1, device_id={"shot": shot, "slab": other}, device_id_type=MESH)

    loads = [
        pltpu.make_async_copy(source, target, load.at[n])
        for n, (source, target) in enumerate(
            (
                (grads_hbm.at[:, :, :, pl.ds(y0, HALF)], mine.at[0]),
                (widths_hbm, widths),
                (tilt_hbm, tilt),
                (model_hbm, model),
                (step_hbm, step),
            )
        )
    ]
    for copy in loads:
        copy.start()

    @pl.when(is_last)
    def _():
        pl.semaphore_wait(there, 1)

    @pl.when(jnp.logical_not(is_last))
    def _():
        pl.semaphore_wait(barrier, 2)

    @pl.when(is_first)
    def _():
        pl.semaphore_signal(there, inc=1, device_id={"shot": shot, "slab": other}, device_id_type=MESH)

    swaps = [
        pltpu.make_async_remote_copy(
            src_ref=grads_hbm.at[p, :, :, pl.ds(y0_other, HALF)], dst_ref=mine.at[1, p],
            send_sem=swap_send.at[p], recv_sem=swap_recv.at[p],
            device_id={"shot": shot, "slab": other}, device_id_type=MESH,
        )
        for p in range(3)
    ]
    for copy in swaps:
        copy.start()

    def place(k):
        p = k // PER_PARAM
        rest = k % PER_PARAM
        b = jnp.where(p == 0, rest // SHOTS, rest % 2)
        slot = jnp.where(p == 0, rest % SHOTS, rest // 2)
        return p, b, slot

    def columns(slot):
        return pl.ds(pl.multiple_of(chunk_of(slot) * ROWS, ROWS), ROWS)

    def send_piece(src, k):
        pltpu.make_async_remote_copy(
            src_ref=src, dst_ref=held.at[k], send_sem=stream_send, recv_sem=stream_recv.at[k],
            device_id={"shot": shot + sign, "slab": slab}, device_id_type=MESH,
        ).start()

    def arrived(k):
        pltpu.make_async_copy(held.at[k], held.at[k], stream_recv.at[k]).wait()

    has = {"low": shot > 0, "high": shot < LAST}
    deep = {"low": slab > 0, "high": slab < SLABS - 1}
    corner[...] = jnp.zeros_like(corner)

    @pl.when(jnp.logical_not(deep["low"]))
    def _():
        rot[:, :, 0:ROWS] = jnp.zeros((2, 3, ROWS, HALF), F32)

    @pl.when(jnp.logical_not(deep["high"]))
    def _():
        rot[:, :, ROWS * (ROWS + 1) :] = jnp.zeros((2, 3, ROWS, HALF), F32)

    def build(t):
        p = t // (NZ // BUILD)
        first = (t % (NZ // BUILD)) * BUILD

        def rows(r, carry):
            lane = lax.broadcasted_iota(jnp.int32, (ROWS, BUILD), 1)
            sub = lax.broadcasted_iota(jnp.int32, (ROWS, BUILD), 0)
            three = widths[:, pl.ds(pl.multiple_of(first, BUILD), BUILD)]
            width_row = jnp.where(p == 0, three[0:1], jnp.where(p == 1, three[1:2], three[2:3]))
            width = jnp.sum(jnp.where(lane == sub + r * ROWS, width_row, 0.0), axis=1, keepdims=True)
            scale = -0.5 / (width * width)
            column = lax.broadcasted_iota(jnp.int32, (ROWS, NZ), 1)
            row = lax.broadcasted_iota(jnp.int32, (ROWS, NZ), 0) + (first + r * ROWS)
            offset = (column - row).astype(F32)
            bell = jnp.exp(offset * offset * scale)
            inverse = 1.0 / jnp.sum(bell, axis=1, keepdims=True)
            r0 = pl.multiple_of(first + r * ROWS, ROWS)
            matrix[p, pl.ds(r0, ROWS), :] = (bell * inverse).astype(BF16)
            return carry

        lax.fori_loop(0, BUILD // ROWS, rows, 0, unroll=UNROLL)

    @pl.when(is_first)
    def _():
        def own_first(k, carry):
            send_piece(grads_hbm.at[0, :, columns(k), pl.ds(y0, HALF)], k)
            return carry

        lax.fori_loop(0, SHOTS, own_first, 0)
        loads[0].wait()
        swaps[0].wait_recv()

        def rest_of_0(k, carry):
            send_piece(mine.at[1, 0, :, columns(k - SHOTS), :], k)
            return carry

        lax.fori_loop(SHOTS, PER_PARAM, rest_of_0, 0)
        for q in range(1, 3):
            swaps[q].wait_recv()

            def both(k, carry):
                p, b, slot = place(k)
                send_piece(mine.at[b, p, :, columns(slot), :], k)
                return carry

            lax.fori_loop(q * PER_PARAM, (q + 1) * PER_PARAM, both, 0)

        def greet(i, carry):
            line = (slab // 2 + i) % (SLABS // 2)
            pl.semaphore_signal(
                barrier, inc=1,
                device_id={"shot": plane_of(half_own, (line // 4) % 2), "slab": 2 * line + half_own},
                device_id_type=MESH,
            )
            return carry

        lax.fori_loop(0, SLABS // 2, greet, 0)
        loads[1].wait()

        def build_step(t, carry):
            build(t)
            return carry

        lax.fori_loop(0, 3 * NZ // BUILD, build_step, 0)

        def smooth(p, carry):
            pltpu.make_async_copy(pencil.at[p], pencil.at[p], part_recv.at[p]).wait()

            def block(b, inner):
                which = (b + slab_x) % (NZ // BLOCK)
                r0 = pl.multiple_of(which * BLOCK, BLOCK)
                value = jnp.dot(matrix[p, pl.ds(r0, BLOCK), :], pencil[p], preferred_element_type=F32)
                d0 = which * (BLOCK // ROWS)
                product[p, pl.ds(d0, BLOCK // ROWS)] = value.astype(BF16).reshape(BLOCK // ROWS, ROWS, QUAD * HALF)

                def to_slab(i, last):
                    d = d0 + (i + slab) % (BLOCK // ROWS)
                    here = (d == slab) & (chunk_own == shot)

                    @pl.when(jnp.logical_not(here))
                    def _():
                        pltpu.make_async_remote_copy(
                            src_ref=product.at[p, d], dst_ref=back.at[half_own, slab_x, p],
                            send_sem=back_send, recv_sem=back_recv,
                            device_id={"shot": chunk_own, "slab": d}, device_id_type=MESH,
                        ).start()

                    @pl.when(here)
                    def _():
                        pltpu.make_async_copy(product.at[p, d], back.at[half_own, slab_x, p], back_recv).start()

                    return last

                lax.fori_loop(0, BLOCK // ROWS, to_slab, 0)
                return inner

            lax.fori_loop(0, NZ // BLOCK, block, 0)
            return carry

        lax.fori_loop(0, 3, smooth, 0)

    @pl.when(jnp.logical_not(is_first))
    def _():
        loads[0].wait()
        loads[1].wait()
        for copy in swaps:
            copy.wait_recv()

    @pl.when(is_middle)
    def _():
        def pass_on(k, carry):
            p, b, slot = place(k)
            arrived(k)
            held[k] = (held[k].astype(F32) + mine[b, p, :, columns(slot), :].astype(F32)).astype(BF16)
            send_piece(held.at[k], k)
            return carry

        lax.fori_loop(0, PIECES, pass_on, 0)

    @pl.when(is_last)
    def _():
        pl.semaphore_wait(barrier, SLABS // 2)

        def finish(k, carry):
            p, b, slot = place(k)
            arrived(k)
            total = held[k].astype(F32) + mine[b, p, :, columns(slot), :].astype(F32)
            turn[...] = total.reshape(ROWS * ROWS, HALF)
            d0 = pl.multiple_of(jnp.where(b == 0, slab, other) * ROWS, ROWS)
            for m in range(QUADS):
                for i in range(QUAD):
                    parts[p, b, slot, m, :, i * HALF : (i + 1) * HALF] = turn[
                        pl.ds(QUAD * m + i, ROWS, stride=ROWS), :
                    ].astype(BF16)
                high = (slot // 4 + m) % 2
                pltpu.make_async_remote_copy(
                    src_ref=parts.at[p, b, slot, m], dst_ref=pencil.at[p, pl.ds(d0, ROWS), :],
                    send_sem=part_send, recv_sem=part_recv.at[p],
                    device_id={
                        "shot": plane_of(core, high),
                        "slab": m * 16 + high * 8 + ((m + slot) % 4) * 2 + 1 - core,
                    },
                    device_id_type=MESH,
                ).start()
            return carry

        lax.fori_loop(0, PIECES, finish, 0)

    for copy in loads[2:]:
        copy.wait()

    def waves(z, carry):
        angle = tilt[z]
        wave[0, z] = jnp.cos(angle)
        wave[1, z] = jnp.sin(angle)
        return carry

    lax.fori_loop(0, ROWS, waves, 0)

    pltpu.make_async_copy(back, back, back_recv).wait()

    for h in range(2):
        ys = slice(h * HALF, (h + 1) * HALF)
        for p in range(3):
            for x in range(ROWS):
                m, i = x // QUAD, x % QUAD
                flat[p, x * ROWS : (x + 1) * ROWS, :] = back[h, m, p, :, i * HALF : (i + 1) * HALF].astype(F32)

        def update(z, carry):
            new = [
                model[p, z, :, ys] - step[p] * flat[p, pl.ds(z, ROWS, stride=ROWS), :]
                for p in range(3)
            ]
            squared = new[0] * new[0]
            along = squared * (1.0 + 2.0 * new[1])
            normal = squared * (1.0 + 2.0 * new[2])
            cosine = wave[0, z, :, ys]
            sine = wave[1, z, :, ys]
            cc = cosine * cosine
            ss = sine * sine
            values = (along * cc + squared * ss, along * ss + squared * cc, (normal - squared) * (sine * cosine))
            for n in range(3):
                r0 = pl.multiple_of((z + 1) * ROWS, ROWS)
                rot[h, n, pl.ds(r0, ROWS), :] = values[n]
            return carry

        lax.fori_loop(0, ROWS, update, 0)
        for n in range(3):
            border[0, n, :, ys] = rot[h, n, pl.ds(ROWS, ROWS, stride=ROWS), :]
            border[1, n, :, ys] = rot[h, n, pl.ds(2 * ROWS - 1, ROWS, stride=ROWS), :]

    for s in range(2):
        for n in range(3):
            corner[s, 0, n : n + 1, :] = border[s, n, 0:1, :]
            corner[s, 1, n : n + 1, :] = border[s, n, ROWS - 1 : ROWS, :]

    moves = []
    for index, (dx, dz) in enumerate(
        ((0, 1), (0, -1), (1, 0), (-1, 0), (1, 1), (1, -1), (-1, 1), (-1, -1))
    ):
        xs = 1 if dx > 0 else 0
        zs = 1 if dz > 0 else 0
        if dx == 0:
            source = rot.at[:, :, pl.ds(ROWS * (ROWS if dz > 0 else 1), ROWS), :]
            target = rot.at[:, :, pl.ds(0 if dz > 0 else ROWS * (ROWS + 1), ROWS), :]
        elif dz == 0:
            source = border.at[xs]
            target = side.at[1 - xs, :, pl.ds(8, ROWS), :]
        else:
            source = corner.at[xs, zs]
            target = near.at[1 - xs, 1 - zs]
        copy = pltpu.make_async_remote_copy(
            src_ref=source, dst_ref=target, send_sem=halo_send.at[index], recv_sem=halo_recv.at[index],
            device_id={"shot": shot + dx, "slab": slab + dz}, device_id_type=MESH,
        )
        goes = (shot + dx >= 0) & (shot + dx < SHOTS) & (slab + dz >= 0) & (slab + dz < SLABS)
        comes = (shot - dx >= 0) & (shot - dx < SHOTS) & (slab - dz >= 0) & (slab - dz < SLABS)
        moves.append((copy, goes, comes, target, dx, dz))

    for copy, goes, comes, target, dx, dz in moves:
        @pl.when(goes)
        def _():
            copy.start()

        if dx != 0:
            @pl.when(jnp.logical_not(comes))
            def _():
                target[...] = jnp.zeros(target.shape, F32)

    for copy in swaps:
        copy.wait_send()

    @pl.when(jnp.logical_not(is_last))
    def _():
        pltpu.make_async_copy(held, held, stream_send).wait()

    @pl.when(is_last)
    def _():
        pltpu.make_async_copy(parts, parts, part_send).wait()

    @pl.when(is_first & (chunk_own == shot))
    def _():
        others = product.at[:, pl.ds(0, SLABS - 1)]
        pltpu.make_async_copy(others, others, back_send).wait()

    @pl.when(is_first & (chunk_own != shot))
    def _():
        pltpu.make_async_copy(product, product, back_send).wait()

    for copy, goes, comes, target, dx, dz in moves:
        @pl.when(comes)
        def _():
            copy.wait_recv()

    for s in range(2):
        for n in range(3):
            side[s, n, 7:8, :] = near[s, 0, n : n + 1, :]
            side[s, n, 8 + ROWS : 9 + ROWS, :] = near[s, 1, n : n + 1, :]
            edge[s, n] = (
                0.25 * (side[s, n, 7 : 7 + ROWS, :] + side[s, n, 9 : 9 + ROWS, :]) + 0.5 * side[s, n, 8 : 8 + ROWS, :]
            )

    def average(group, carry):
        x_at = lax.broadcasted_iota(jnp.int32, (ROWS, HALF), 0)
        z0 = pl.multiple_of(group * 8, 8)
        for n in range(3):
            for h in range(2):
                ys = slice(h * HALF, (h + 1) * HALF)
                low = edge[0, n, pl.ds(z0, 8), ys]
                high = edge[1, n, pl.ds(z0, 8), ys]
                for i in range(8):
                    three = [
                        rot[h, n, pl.ds(pl.multiple_of((z0 + i + j) * ROWS, ROWS), ROWS), :] for j in range(3)
                    ]
                    mean = 0.25 * (three[0] + three[2]) + 0.5 * three[1]
                    before = jnp.where(x_at == 0, low[i : i + 1], pltpu.roll(mean, 1, 0))
                    after = jnp.where(x_at == ROWS - 1, high[i : i + 1], pltpu.roll(mean, ROWS - 1, 0))
                    out[n, z0 + i, :, ys] = 0.25 * (before + after) + 0.5 * mean
        return carry

    lax.fori_loop(0, ROWS // 8, average, 0)

    for copy, goes, comes, target, dx, dz in moves:
        @pl.when(goes)
        def _():
            copy.wait_send()


def shards(partial_grads, model, tilt, widths, step_length):
    vmem = pl.BlockSpec(memory_space=pltpu.VMEM)
    hbm = pl.BlockSpec(memory_space=pl.ANY)
    wide = 2 * HALF
    return pl.pallas_call(
        kernel,
        out_shape=jax.ShapeDtypeStruct(model.shape, F32),
        in_specs=[hbm] * 5,
        out_specs=vmem,
        scratch_shapes=[
            pltpu.VMEM((2, 3, ROWS, SHOTS * ROWS, HALF), BF16),
            pltpu.VMEM(model.shape, F32),
            pltpu.VMEM(tilt.shape, F32),
            pltpu.VMEM(widths.shape, F32),
            pltpu.SMEM(step_length.shape, F32),
            pltpu.VMEM((PIECES, ROWS, ROWS, HALF), BF16),
            pltpu.VMEM((ROWS * ROWS, HALF), F32),
            pltpu.VMEM((3, 2, SHOTS, QUADS, ROWS, QUAD * HALF), BF16),
            pltpu.VMEM((3, NZ, QUAD * HALF), BF16),
            pltpu.VMEM((3, NZ, NZ), BF16),
            pltpu.VMEM((3, SLABS, ROWS, QUAD * HALF), BF16),
            pltpu.VMEM((2, QUADS, 3, ROWS, QUAD * HALF), BF16),
            pltpu.VMEM((3, ROWS * ROWS, HALF), F32),
            pltpu.VMEM((2, ROWS, ROWS, wide), F32),
            pltpu.VMEM((2, 3, (ROWS + 2) * ROWS, HALF), F32),
            pltpu.VMEM((2, 3, ROWS, wide), F32),
            pltpu.VMEM((2, 2, 8, wide), F32),
            pltpu.VMEM((2, 3, 2 * ROWS, wide), F32),
            pltpu.VMEM((2, 2, 8, wide), F32),
            pltpu.VMEM((2, 3, ROWS, wide), F32),
            pltpu.SemaphoreType.REGULAR,
            pltpu.SemaphoreType.DMA((5,)),
            pltpu.SemaphoreType.DMA((3,)),
            pltpu.SemaphoreType.DMA((3,)),
            pltpu.SemaphoreType.DMA,
            pltpu.SemaphoreType.DMA((PIECES,)),
            pltpu.SemaphoreType.DMA,
            pltpu.SemaphoreType.DMA((3,)),
            pltpu.SemaphoreType.DMA,
            pltpu.SemaphoreType.DMA,
            pltpu.SemaphoreType.DMA((8,)),
            pltpu.SemaphoreType.DMA((8,)),
        ],
        compiler_params=pltpu.CompilerParams(
            collective_id=0, has_side_effects=True, vmem_limit_bytes=60 * 1024 * 1024
        ),
    )(partial_grads[0], model, tilt, widths, step_length)


def solution(mesh):
    placed = (
        P("shot", None, "slab", None, None),
        P(None, "slab", "shot", None),
        P("slab", "shot", None),
        P(),
        P(),
    )
    return jax.shard_map(
        shards, mesh=mesh, in_specs=placed, out_specs=P(None, "slab", "shot", None), check_vma=False
    )
```

```python
import jax
import jax.numpy as jnp
from jax import lax
from jax.experimental import pallas as pl
from jax.experimental.pallas import tpu as pltpu
from jax.sharding import PartitionSpec as P

MESH = pl.DeviceIdType.MESH
F32 = jnp.float32
BF16 = jnp.bfloat16

SHOTS = 8
SLABS = 64
LAST = SHOTS - 1
ROWS = 16
HALF = 128
NZ = ROWS * SLABS
PIECE = 8
SPLIT = ROWS // PIECE
PER_PARAM = SHOTS * SPLIT
PIECES = 3 * PER_PARAM
SKEW = 11
LAG = 16
BLOCK = 256
UNROLL = 4
FILL = (SKEW * LAST) // 2
GREET_STEPS = (SLABS - 1) // 3
BUILD = 128
STEPS_BUILD = 3 * NZ // BUILD


def chunk_of(slot):
    return slot // 2 + (slot % 2) * (LAST - 2 * (slot // 2))


def owner_slab(pair, slot):
    return (pair % 4) * 16 + (pair // 4) * 8 + ((pair + slot) % 4) * 2 + slot // 4


def kernel(
    grads_hbm, model_hbm, tilt_hbm, widths_hbm, step_hbm, out,
    grads, model, tilt, widths, step, held, turn, parts, pencil, matrix, product, back, flat, wave, rot, border, corner, side, near, edge,
    there, load, stream_send, stream_recv, part_send, part_recv, back_send, back_recv, halo_send, halo_recv,
):
    shot = lax.axis_index("shot")
    slab = lax.axis_index("slab")
    upper = (slab // 8) % 2
    rank_0 = shot + upper * (LAST - 2 * shot)
    sign_0 = 1 - 2 * upper
    ranks = (rank_0, LAST - rank_0)
    signs = (sign_0, -sign_0)
    is_end = (rank_0 == 0) | (rank_0 == LAST)
    end_half = jnp.where(rank_0 == LAST, 0, 1)
    slab_x, slab_y = slab // 16, (slab // 2) % 4
    slot_own = (slab_y + 4 - slab_x) % 4 + 4 * (slab % 2)
    pair_own = slab_x + 4 * upper
    chunk_own = chunk_of(slot_own)

    def owner_of(h, g):
        high = (g // 8) % 2
        flip = high + h - 2 * high * h
        return LAST - LAST * flip

    loads = [
        pltpu.make_async_copy(source, target, load.at[n])
        for n, (source, target) in enumerate(
            ((grads_hbm, grads), (widths_hbm, widths), (tilt_hbm, tilt), (model_hbm, model), (step_hbm, step))
        )
    ]
    barrier = pltpu.get_barrier_semaphore()

    for to in (-1, 1):
        @pl.when((shot + to >= 0) & (shot + to < SHOTS) & (rank_0 + sign_0 * to > 0) & (rank_0 + sign_0 * to < LAST))
        def _():
            pl.semaphore_signal(barrier, inc=1, device_id={"shot": shot + to, "slab": slab}, device_id_type=MESH)

    def greet(i, carry):
        g = (slab + i) % SLABS
        pl.semaphore_signal(
            barrier, inc=1, device_id={"shot": owner_of(end_half, g), "slab": g}, device_id_type=MESH
        )
        return carry

    for copy in loads:
        copy.start()

    has = {"low": shot > 0, "high": shot < LAST}
    deep = {"low": slab > 0, "high": slab < SLABS - 1}
    corner[...] = jnp.zeros_like(corner)

    @pl.when(jnp.logical_not(deep["low"]))
    def _():
        rot[:, :, 0:ROWS] = jnp.zeros((2, 3, ROWS, HALF), F32)

    @pl.when(jnp.logical_not(deep["high"]))
    def _():
        rot[:, :, ROWS * (ROWS + 1) :] = jnp.zeros((2, 3, ROWS, HALF), F32)

    def send_piece(src, h, k):
        pltpu.make_async_remote_copy(
            src_ref=src, dst_ref=held.at[h, k], send_sem=stream_send.at[h], recv_sem=stream_recv.at[h, k],
            device_id={"shot": shot + signs[h], "slab": slab}, device_id_type=MESH,
        ).start()

    def piece(h, k, starts):
        rank = ranks[h]
        p = k // PER_PARAM
        rest = k % PER_PARAM
        slot = rest // SPLIT
        chunk = chunk_of(slot)
        z0 = (rest % SPLIT) * PIECE
        x0 = pl.multiple_of(chunk * ROWS, ROWS)
        where = (p, pl.ds(z0, PIECE), pl.ds(x0, ROWS), pl.ds(h * HALF, HALF))
        own = grads.at[where]

        if starts:
            send_piece(grads_hbm.at[where], h, k)
            return
        pltpu.make_async_copy(held.at[h, k], held.at[h, k], stream_recv.at[h, k]).wait()

        @pl.when(rank < LAST)
        def _():
            held[h, k] = (held[h, k].astype(F32) + own[...].astype(F32)).astype(BF16)
            send_piece(held.at[h, k], h, k)

        @pl.when(rank == LAST)
        def _():
            total = held[h, k].astype(F32) + own[...].astype(F32)
            r0 = pl.multiple_of(z0 * ROWS, PIECE * ROWS)
            turn[pl.ds(r0, PIECE * ROWS), :] = total.reshape(PIECE * ROWS, HALF)

            @pl.when(rest % SPLIT == SPLIT - 1)
            def _():
                for j in range(8):
                    g = owner_slab(j, slot)
                    for i in range(2):
                        parts[p, g, :, i * HALF : (i + 1) * HALF] = turn[
                            pl.ds(2 * j + i, ROWS, stride=ROWS), :
                        ].astype(BF16)

                def to_owner(i, carry):
                    g = owner_slab((i + slab) % 8, slot)
                    d0 = pl.multiple_of(slab * ROWS, ROWS)

                    @pl.when(g != slab)
                    def _():
                        pltpu.make_async_remote_copy(
                            src_ref=parts.at[p, g], dst_ref=pencil.at[p, pl.ds(d0, ROWS), :],
                            send_sem=part_send, recv_sem=part_recv.at[p],
                            device_id={"shot": owner_of(h, g), "slab": g}, device_id_type=MESH,
                        ).start()

                    @pl.when(g == slab)
                    def _():
                        pltpu.make_async_copy(
                            parts.at[p, g], pencil.at[p, pl.ds(d0, ROWS), :], part_recv.at[p]
                        ).start()

                    return carry

                lax.fori_loop(0, 8, to_owner, 0)

    def build(t):
        p = t // (NZ // BUILD)
        first = (t % (NZ // BUILD)) * BUILD

        def rows(r, carry):
            lane = lax.broadcasted_iota(jnp.int32, (ROWS, BUILD), 1)
            sub = lax.broadcasted_iota(jnp.int32, (ROWS, BUILD), 0)
            three = widths[:, pl.ds(pl.multiple_of(first, BUILD), BUILD)]
            width_row = jnp.where(p == 0, three[0:1], jnp.where(p == 1, three[1:2], three[2:3]))
            width = jnp.sum(jnp.where(lane == sub + r * ROWS, width_row, 0.0), axis=1, keepdims=True)
            scale = -0.5 / (width * width)
            column = lax.broadcasted_iota(jnp.int32, (ROWS, NZ), 1)
            row = lax.broadcasted_iota(jnp.int32, (ROWS, NZ), 0) + (first + r * ROWS)
            offset = (column - row).astype(F32)
            bell = jnp.exp(offset * offset * scale)
            inverse = 1.0 / jnp.sum(bell, axis=1, keepdims=True)
            r0 = pl.multiple_of(first + r * ROWS, ROWS)
            matrix[p, pl.ds(r0, ROWS), :] = (bell * inverse).astype(BF16)
            return carry

        lax.fori_loop(0, BUILD // ROWS, rows, 0, unroll=UNROLL)

    def smooth(p):
        pltpu.make_async_copy(pencil.at[p], pencil.at[p], part_recv.at[p]).wait()

        def block(b, carry):
            which = (b + slab // ROWS) % (NZ // BLOCK)
            r0 = pl.multiple_of(which * BLOCK, BLOCK)
            value = jnp.dot(matrix[p, pl.ds(r0, BLOCK), :], pencil[p], preferred_element_type=F32)
            d0 = which * (BLOCK // ROWS)
            product[p, pl.ds(d0, BLOCK // ROWS)] = value.astype(BF16).reshape(BLOCK // ROWS, ROWS, 2 * HALF)

            def to_slab(i, inner):
                d = d0 + (i + upper) % 2 * 8 + (i // 2 + slab) % 8
                here = (d == slab) & (chunk_own == shot)

                @pl.when(jnp.logical_not(here))
                def _():
                    pltpu.make_async_remote_copy(
                        src_ref=product.at[p, d], dst_ref=back.at[end_half, pair_own, p],
                        send_sem=back_send, recv_sem=back_recv,
                        device_id={"shot": chunk_own, "slab": d}, device_id_type=MESH,
                    ).start()

                @pl.when(here)
                def _():
                    pltpu.make_async_copy(
                        product.at[p, d], back.at[end_half, pair_own, p], back_recv
                    ).start()

                return inner

            lax.fori_loop(0, BLOCK // ROWS, to_slab, 0)
            return carry

        lax.fori_loop(0, NZ // BLOCK, block, 0)

    @pl.when(jnp.logical_not(is_end))
    def _():
        pl.semaphore_wait(barrier, 2)

    for to in (-1, 1):
        @pl.when((shot + to >= 0) & (shot + to < SHOTS) & ((rank_0 + sign_0 * to == 0) | (rank_0 + sign_0 * to == LAST)))
        def _():
            pl.semaphore_signal(there, inc=1, device_id={"shot": shot + to, "slab": slab}, device_id_type=MESH)

    @pl.when(is_end)
    def _():
        pl.semaphore_wait(there, 1)

    def at_step(t, carry):
        for h in range(2):
            rank = ranks[h]
            k = t - (SKEW * rank) // 2

            @pl.when((rank == 0) & (t < PIECES // 2))
            def _():
                piece(h, 2 * t, True)
                piece(h, 2 * t + 1, True)

            if h == 0:
                @pl.when(t == 0)
                def _():
                    loads[0].wait()
                    loads[1].wait()

            @pl.when((rank > 0) & (k >= 0) & (k < PIECES))
            def _():
                piece(h, k, False)

        @pl.when(is_end & (t < GREET_STEPS))
        def _():
            lax.fori_loop(1 + 3 * t, 4 + 3 * t, greet, 0)

        @pl.when(is_end & (t < STEPS_BUILD))
        def _():
            build(t)

        @pl.when(is_end & (t == FILL - 1))
        def _():
            pl.semaphore_wait(barrier, SLABS - 1)

        after = t - FILL - SPLIT * (slot_own + 1) - LAG

        @pl.when(is_end & (after >= 0) & (after % PER_PARAM == 0) & (after < PIECES))
        def _():
            smooth(after // PER_PARAM)

        return carry

    lax.fori_loop(0, FILL + PIECES + LAG + 1, at_step, 0)

    for copy in loads[2:]:
        copy.wait()

    def waves(z, carry):
        angle = tilt[z]
        wave[0, z] = jnp.cos(angle)
        wave[1, z] = jnp.sin(angle)
        return carry

    lax.fori_loop(0, ROWS, waves, 0)

    pltpu.make_async_copy(back, back, back_recv).wait()

    for h in range(2):
        for p in range(3):
            for j in range(8):
                for i in range(2):
                    x = 2 * j + i
                    flat[h, p, x * ROWS : (x + 1) * ROWS, :] = back[h, j, p, :, i * HALF : (i + 1) * HALF].astype(F32)

    def update(z, h):
        ys = slice(h * HALF, (h + 1) * HALF)
        new = [
            model[p, z, :, ys] - step[p] * flat[h, p, pl.ds(z, ROWS, stride=ROWS), :]
            for p in range(3)
        ]
        squared = new[0] * new[0]
        along = squared * (1.0 + 2.0 * new[1])
        normal = squared * (1.0 + 2.0 * new[2])
        cosine = wave[0, z, :, ys]
        sine = wave[1, z, :, ys]
        cc = cosine * cosine
        ss = sine * sine
        values = (along * cc + squared * ss, along * ss + squared * cc, (normal - squared) * (sine * cosine))
        r0 = (z + 1) * ROWS
        if not isinstance(z, int):
            r0 = pl.multiple_of(r0, ROWS)
        for n in range(3):
            rot[h, n, pl.ds(r0, ROWS), :] = values[n]

    for h in range(2):
        ys = slice(h * HALF, (h + 1) * HALF)
        for zs, z in enumerate((0, ROWS - 1)):
            update(z, h)
            for xs, x in enumerate((0, ROWS - 1)):
                r0 = (z + 1) * ROWS + x
                for n in range(3):
                    corner[xs, zs, n : n + 1, ys] = rot[h, n, r0 : r0 + 1, :]

    moves = []
    for index, (dx, dz) in enumerate(
        ((0, 1), (0, -1), (1, 0), (-1, 0), (1, 1), (1, -1), (-1, 1), (-1, -1))
    ):
        xs = 1 if dx > 0 else 0
        zs = 1 if dz > 0 else 0
        if dx == 0:
            source = rot.at[:, :, pl.ds(ROWS * (ROWS if dz > 0 else 1), ROWS), :]
            target = rot.at[:, :, pl.ds(0 if dz > 0 else ROWS * (ROWS + 1), ROWS), :]
        elif dz == 0:
            source = border.at[xs]
            target = side.at[1 - xs, :, pl.ds(8, ROWS), :]
        else:
            source = corner.at[xs, zs]
            target = near.at[1 - xs, 1 - zs]
        copy = pltpu.make_async_remote_copy(
            src_ref=source, dst_ref=target, send_sem=halo_send.at[index], recv_sem=halo_recv.at[index],
            device_id={"shot": shot + dx, "slab": slab + dz}, device_id_type=MESH,
        )
        goes = (shot + dx >= 0) & (shot + dx < SHOTS) & (slab + dz >= 0) & (slab + dz < SLABS)
        comes = (shot - dx >= 0) & (shot - dx < SHOTS) & (slab - dz >= 0) & (slab - dz < SLABS)
        moves.append((copy, goes, comes, target, dx, dz))

    for copy, goes, comes, target, dx, dz in moves:
        if dz != 0:
            @pl.when(goes)
            def _():
                copy.start()

    def update_both(z, carry):
        update(z, 0)
        update(z, 1)
        return carry

    lax.fori_loop(1, ROWS - 1, update_both, 0)
    for h in range(2):
        ys = slice(h * HALF, (h + 1) * HALF)
        for n in range(3):
            border[0, n, :, ys] = rot[h, n, pl.ds(ROWS, ROWS, stride=ROWS), :]
            border[1, n, :, ys] = rot[h, n, pl.ds(2 * ROWS - 1, ROWS, stride=ROWS), :]

    for copy, goes, comes, target, dx, dz in moves:
        if dz == 0:
            @pl.when(goes)
            def _():
                copy.start()

        if dx != 0:
            @pl.when(jnp.logical_not(comes))
            def _():
                target[...] = jnp.zeros(target.shape, F32)

    for h in range(2):
        @pl.when(ranks[h] < LAST)
        def _():
            pltpu.make_async_copy(held.at[h], held.at[h], stream_send.at[h]).wait()

    @pl.when(is_end)
    def _():
        others = parts.at[:, pl.ds(0, SLABS - 1)]
        pltpu.make_async_copy(others, others, part_send).wait()

    @pl.when(is_end & (chunk_own == shot))
    def _():
        others = product.at[:, pl.ds(0, SLABS - 1)]
        pltpu.make_async_copy(others, others, back_send).wait()

    @pl.when(is_end & (chunk_own != shot))
    def _():
        pltpu.make_async_copy(product, product, back_send).wait()

    for copy, goes, comes, target, dx, dz in moves:
        @pl.when(comes)
        def _():
            copy.wait_recv()

    for s in range(2):
        for n in range(3):
            side[s, n, 7:8, :] = near[s, 0, n : n + 1, :]
            side[s, n, 8 + ROWS : 9 + ROWS, :] = near[s, 1, n : n + 1, :]
            edge[s, n] = (
                0.25 * (side[s, n, 7 : 7 + ROWS, :] + side[s, n, 9 : 9 + ROWS, :]) + 0.5 * side[s, n, 8 : 8 + ROWS, :]
            )

    def average(group, carry):
        x_at = lax.broadcasted_iota(jnp.int32, (ROWS, HALF), 0)
        z0 = pl.multiple_of(group * 8, 8)
        for n in range(3):
            for h in range(2):
                ys = slice(h * HALF, (h + 1) * HALF)
                low = edge[0, n, pl.ds(z0, 8), ys]
                high = edge[1, n, pl.ds(z0, 8), ys]
                for i in range(8):
                    three = [
                        rot[h, n, pl.ds(pl.multiple_of((z0 + i + j) * ROWS, ROWS), ROWS), :] for j in range(3)
                    ]
                    mean = 0.25 * (three[0] + three[2]) + 0.5 * three[1]
                    before = jnp.where(x_at == 0, low[i : i + 1], pltpu.roll(mean, 1, 0))
                    after = jnp.where(x_at == ROWS - 1, high[i : i + 1], pltpu.roll(mean, ROWS - 1, 0))
                    out[n, z0 + i, :, ys] = 0.25 * (before + after) + 0.5 * mean
        return carry

    lax.fori_loop(0, ROWS // 8, average, 0)

    for copy, goes, comes, target, dx, dz in moves:
        @pl.when(goes)
        def _():
            copy.wait_send()


def shards(partial_grads, model, tilt, widths, step_length):
    vmem = pl.BlockSpec(memory_space=pltpu.VMEM)
    hbm = pl.BlockSpec(memory_space=pl.ANY)
    wide = 2 * HALF
    return pl.pallas_call(
        kernel,
        out_shape=jax.ShapeDtypeStruct(model.shape, F32),
        in_specs=[hbm] * 5,
        out_specs=vmem,
        scratch_shapes=[
            pltpu.VMEM(partial_grads.shape[1:], BF16),
            pltpu.VMEM(model.shape, F32),
            pltpu.VMEM(tilt.shape, F32),
            pltpu.VMEM(widths.shape, F32),
            pltpu.SMEM(step_length.shape, F32),
            pltpu.VMEM((2, PIECES, PIECE, ROWS, HALF), BF16),
            pltpu.VMEM((ROWS * ROWS, HALF), F32),
            pltpu.VMEM((3, SLABS, ROWS, wide), BF16),
            pltpu.VMEM((3, NZ, wide), BF16),
            pltpu.VMEM((3, NZ, NZ), BF16),
            pltpu.VMEM((3, SLABS, ROWS, wide), BF16),
            pltpu.VMEM((2, 8, 3, ROWS, wide), BF16),
            pltpu.VMEM((2, 3, ROWS * ROWS, HALF), F32),
            pltpu.VMEM((2, ROWS, ROWS, wide), F32),
            pltpu.VMEM((2, 3, (ROWS + 2) * ROWS, HALF), F32),
            pltpu.VMEM((2, 3, ROWS, wide), F32),
            pltpu.VMEM((2, 2, 8, wide), F32),
            pltpu.VMEM((2, 3, 2 * ROWS, wide), F32),
            pltpu.VMEM((2, 2, 8, wide), F32),
            pltpu.VMEM((2, 3, ROWS, wide), F32),
            pltpu.SemaphoreType.REGULAR,
            pltpu.SemaphoreType.DMA((5,)),
            pltpu.SemaphoreType.DMA((2,)),
            pltpu.SemaphoreType.DMA((2, PIECES)),
            pltpu.SemaphoreType.DMA,
            pltpu.SemaphoreType.DMA((3,)),
            pltpu.SemaphoreType.DMA,
            pltpu.SemaphoreType.DMA,
            pltpu.SemaphoreType.DMA((8,)),
            pltpu.SemaphoreType.DMA((8,)),
        ],
        compiler_params=pltpu.CompilerParams(
            collective_id=0, has_side_effects=True, vmem_limit_bytes=60 * 1024 * 1024
        ),
    )(partial_grads[0], model, tilt, widths, step_length)


def solution(mesh):
    placed = (
        P("shot", None, "slab", None, None),
        P(None, "slab", "shot", None),
        P("slab", "shot", None),
        P(),
        P(),
    )
    return jax.shard_map(
        shards, mesh=mesh, in_specs=placed, out_specs=P(None, "slab", "shot", None), check_vma=False
    )
```

```python
import jax
import jax.numpy as jnp
from jax import lax
from jax.experimental import pallas as pl
from jax.experimental.pallas import tpu as pltpu
from jax.sharding import PartitionSpec as P

MESH = pl.DeviceIdType.MESH
F32 = jnp.float32
BF16 = jnp.bfloat16

SHOTS = 8
SLABS = 64
LAST = SHOTS - 1
ROWS = 16
HALF = 128
NZ = ROWS * SLABS
PIECE = 8
SPLIT = ROWS // PIECE
PER_PARAM = SHOTS * SPLIT
PIECES = 3 * PER_PARAM
SKEW = 11
LAG = 16
BLOCK = 256
UNROLL = 4
FILL = (SKEW * LAST) // 2
GREET_STEPS = (SLABS - 1) // 3
BUILD = 128
STEPS_BUILD = 3 * NZ // BUILD


def chunk_of(slot):
    return slot // 2 + (slot % 2) * (LAST - 2 * (slot // 2))


def owner_slab(pair, slot):
    return (pair % 4) * 16 + (pair // 4) * 8 + ((pair + slot) % 4) * 2 + slot // 4


def kernel(
    grads_hbm, model_hbm, tilt_hbm, widths_hbm, step_hbm, out,
    grads, model, tilt, widths, step, held, turn, parts, pencil, matrix, product, back, flat, wave, rot, border, corner, side, near, edge,
    there, load, stream_send, stream_recv, part_send, part_recv, back_send, back_recv, halo_send, halo_recv,
):
    shot = lax.axis_index("shot")
    slab = lax.axis_index("slab")
    upper = (slab // 8) % 2
    rank_0 = shot + upper * (LAST - 2 * shot)
    sign_0 = 1 - 2 * upper
    ranks = (rank_0, LAST - rank_0)
    signs = (sign_0, -sign_0)
    is_end = (rank_0 == 0) | (rank_0 == LAST)
    end_half = jnp.where(rank_0 == LAST, 0, 1)
    slab_x, slab_y = slab // 16, (slab // 2) % 4
    slot_own = (slab_y + 4 - slab_x) % 4 + 4 * (slab % 2)
    pair_own = slab_x + 4 * upper
    chunk_own = chunk_of(slot_own)

    def owner_of(h, g):
        high = (g // 8) % 2
        flip = high + h - 2 * high * h
        return LAST - LAST * flip

    loads = [
        pltpu.make_async_copy(source, target, load.at[n])
        for n, (source, target) in enumerate(
            ((grads_hbm, grads), (widths_hbm, widths), (tilt_hbm, tilt), (model_hbm, model), (step_hbm, step))
        )
    ]
    barrier = pltpu.get_barrier_semaphore()

    for to in (-1, 1):
        @pl.when((shot + to >= 0) & (shot + to < SHOTS) & (rank_0 + sign_0 * to > 0) & (rank_0 + sign_0 * to < LAST))
        def _():
            pl.semaphore_signal(barrier, inc=1, device_id={"shot": shot + to, "slab": slab}, device_id_type=MESH)

    def greet(i, carry):
        g = (slab + i) % SLABS
        pl.semaphore_signal(
            barrier, inc=1, device_id={"shot": owner_of(end_half, g), "slab": g}, device_id_type=MESH
        )
        return carry

    for copy in loads:
        copy.start()

    has = {"low": shot > 0, "high": shot < LAST}
    deep = {"low": slab > 0, "high": slab < SLABS - 1}
    corner[...] = jnp.zeros_like(corner)

    @pl.when(jnp.logical_not(deep["low"]))
    def _():
        rot[:, :, 0:ROWS] = jnp.zeros((2, 3, ROWS, HALF), F32)

    @pl.when(jnp.logical_not(deep["high"]))
    def _():
        rot[:, :, ROWS * (ROWS + 1) :] = jnp.zeros((2, 3, ROWS, HALF), F32)

    def send_piece(src, h, k):
        pltpu.make_async_remote_copy(
            src_ref=src, dst_ref=held.at[h, k], send_sem=stream_send.at[h], recv_sem=stream_recv.at[h, k],
            device_id={"shot": shot + signs[h], "slab": slab}, device_id_type=MESH,
        ).start()

    def piece(h, k, starts):
        rank = ranks[h]
        p = k // PER_PARAM
        rest = k % PER_PARAM
        slot = rest // SPLIT
        chunk = chunk_of(slot)
        z0 = (rest % SPLIT) * PIECE
        x0 = pl.multiple_of(chunk * ROWS, ROWS)
        where = (p, pl.ds(z0, PIECE), pl.ds(x0, ROWS), pl.ds(h * HALF, HALF))
        own = grads.at[where]

        if starts:
            send_piece(grads_hbm.at[where], h, k)
            return
        pltpu.make_async_copy(held.at[h, k], held.at[h, k], stream_recv.at[h, k]).wait()

        @pl.when(rank < LAST)
        def _():
            held[h, k] = (held[h, k].astype(F32) + own[...].astype(F32)).astype(BF16)
            send_piece(held.at[h, k], h, k)

        @pl.when(rank == LAST)
        def _():
            total = held[h, k].astype(F32) + own[...].astype(F32)
            r0 = pl.multiple_of(z0 * ROWS, PIECE * ROWS)
            turn[pl.ds(r0, PIECE * ROWS), :] = total.reshape(PIECE * ROWS, HALF)

            @pl.when(rest % SPLIT == SPLIT - 1)
            def _():
                for j in range(8):
                    g = owner_slab(j, slot)
                    for i in range(2):
                        parts[p, g, :, i * HALF : (i + 1) * HALF] = turn[
                            pl.ds(2 * j + i, ROWS, stride=ROWS), :
                        ].astype(BF16)

                def to_owner(i, carry):
                    g = owner_slab((i + slab) % 8, slot)
                    d0 = pl.multiple_of(slab * ROWS, ROWS)

                    @pl.when(g != slab)
                    def _():
                        pltpu.make_async_remote_copy(
                            src_ref=parts.at[p, g], dst_ref=pencil.at[p, pl.ds(d0, ROWS), :],
                            send_sem=part_send, recv_sem=part_recv.at[p],
                            device_id={"shot": owner_of(h, g), "slab": g}, device_id_type=MESH,
                        ).start()

                    @pl.when(g == slab)
                    def _():
                        pltpu.make_async_copy(
                            parts.at[p, g], pencil.at[p, pl.ds(d0, ROWS), :], part_recv.at[p]
                        ).start()

                    return carry

                lax.fori_loop(0, 8, to_owner, 0)

    def build(t):
        p = t // (NZ // BUILD)
        first = (t % (NZ // BUILD)) * BUILD

        def rows(r, carry):
            lane = lax.broadcasted_iota(jnp.int32, (ROWS, BUILD), 1)
            sub = lax.broadcasted_iota(jnp.int32, (ROWS, BUILD), 0)
            three = widths[:, pl.ds(pl.multiple_of(first, BUILD), BUILD)]
            width_row = jnp.where(p == 0, three[0:1], jnp.where(p == 1, three[1:2], three[2:3]))
            width = jnp.sum(jnp.where(lane == sub + r * ROWS, width_row, 0.0), axis=1, keepdims=True)
            scale = -0.5 / (width * width)
            column = lax.broadcasted_iota(jnp.int32, (ROWS, NZ), 1)
            row = lax.broadcasted_iota(jnp.int32, (ROWS, NZ), 0) + (first + r * ROWS)
            offset = (column - row).astype(F32)
            bell = jnp.exp(offset * offset * scale)
            inverse = 1.0 / jnp.sum(bell, axis=1, keepdims=True)
            r0 = pl.multiple_of(first + r * ROWS, ROWS)
            matrix[p, pl.ds(r0, ROWS), :] = (bell * inverse).astype(BF16)
            return carry

        lax.fori_loop(0, BUILD // ROWS, rows, 0, unroll=UNROLL)

    def smooth(p):
        pltpu.make_async_copy(pencil.at[p], pencil.at[p], part_recv.at[p]).wait()

        def block(b, carry):
            which = (b + slab // ROWS) % (NZ // BLOCK)
            r0 = pl.multiple_of(which * BLOCK, BLOCK)
            value = jnp.dot(matrix[p, pl.ds(r0, BLOCK), :], pencil[p], preferred_element_type=F32)
            d0 = which * (BLOCK // ROWS)
            product[p, pl.ds(d0, BLOCK // ROWS)] = value.astype(BF16).reshape(BLOCK // ROWS, ROWS, 2 * HALF)

            def to_slab(i, inner):
                d = d0 + (i + upper) % 2 * 8 + (i // 2 + slab) % 8
                here = (d == slab) & (chunk_own == shot)

                @pl.when(jnp.logical_not(here))
                def _():
                    pltpu.make_async_remote_copy(
                        src_ref=product.at[p, d], dst_ref=back.at[end_half, pair_own, p],
                        send_sem=back_send, recv_sem=back_recv.at[p],
                        device_id={"shot": chunk_own, "slab": d}, device_id_type=MESH,
                    ).start()

                @pl.when(here)
                def _():
                    pltpu.make_async_copy(
                        product.at[p, d], back.at[end_half, pair_own, p], back_recv.at[p]
                    ).start()

                return inner

            lax.fori_loop(0, BLOCK // ROWS, to_slab, 0)
            return carry

        lax.fori_loop(0, NZ // BLOCK, block, 0)

    @pl.when(jnp.logical_not(is_end))
    def _():
        pl.semaphore_wait(barrier, 2)

    for to in (-1, 1):
        @pl.when((shot + to >= 0) & (shot + to < SHOTS) & ((rank_0 + sign_0 * to == 0) | (rank_0 + sign_0 * to == LAST)))
        def _():
            pl.semaphore_signal(there, inc=1, device_id={"shot": shot + to, "slab": slab}, device_id_type=MESH)

    @pl.when(is_end)
    def _():
        pl.semaphore_wait(there, 1)

    def at_step(t, carry):
        for h in range(2):
            rank = ranks[h]
            k = t - (SKEW * rank) // 2

            @pl.when((rank == 0) & (t < PIECES // 2))
            def _():
                piece(h, 2 * t, True)
                piece(h, 2 * t + 1, True)

            if h == 0:
                @pl.when(t == 0)
                def _():
                    loads[0].wait()
                    loads[1].wait()

            @pl.when((rank > 0) & (k >= 0) & (k < PIECES))
            def _():
                piece(h, k, False)

        @pl.when(is_end & (t < GREET_STEPS))
        def _():
            lax.fori_loop(1 + 3 * t, 4 + 3 * t, greet, 0)

        @pl.when(is_end & (t < STEPS_BUILD))
        def _():
            build(t)

        @pl.when(is_end & (t == FILL - 1))
        def _():
            pl.semaphore_wait(barrier, SLABS - 1)

        after = t - FILL - SPLIT * (slot_own + 1) - LAG

        @pl.when(is_end & (after >= 0) & (after % PER_PARAM == 0) & (after < PIECES))
        def _():
            smooth(after // PER_PARAM)

        return carry

    lax.fori_loop(0, FILL + PIECES + LAG + 1, at_step, 0)

    for copy in loads[2:]:
        copy.wait()

    def waves(z, carry):
        angle = tilt[z]
        wave[0, z] = jnp.cos(angle)
        wave[1, z] = jnp.sin(angle)
        return carry

    lax.fori_loop(0, ROWS, waves, 0)

    for p in range(3):
        landed = back.at[:, :, p]
        pltpu.make_async_copy(landed, landed, back_recv.at[p]).wait()
        for h in range(2):
            for j in range(8):
                for i in range(2):
                    x = 2 * j + i
                    flat[h, p, x * ROWS : (x + 1) * ROWS, :] = back[h, j, p, :, i * HALF : (i + 1) * HALF].astype(F32)

    def update(z, h):
        ys = slice(h * HALF, (h + 1) * HALF)
        new = [
            model[p, z, :, ys] - step[p] * flat[h, p, pl.ds(z, ROWS, stride=ROWS), :]
            for p in range(3)
        ]
        squared = new[0] * new[0]
        along = squared * (1.0 + 2.0 * new[1])
        normal = squared * (1.0 + 2.0 * new[2])
        cosine = wave[0, z, :, ys]
        sine = wave[1, z, :, ys]
        cc = cosine * cosine
        ss = sine * sine
        values = (along * cc + squared * ss, along * ss + squared * cc, (normal - squared) * (sine * cosine))
        r0 = (z + 1) * ROWS
        if not isinstance(z, int):
            r0 = pl.multiple_of(r0, ROWS)
        for n in range(3):
            rot[h, n, pl.ds(r0, ROWS), :] = values[n]

    for h in range(2):
        ys = slice(h * HALF, (h + 1) * HALF)
        for zs, z in enumerate((0, ROWS - 1)):
            update(z, h)
            for xs, x in enumerate((0, ROWS - 1)):
                r0 = (z + 1) * ROWS + x
                for n in range(3):
                    corner[xs, zs, n : n + 1, ys] = rot[h, n, r0 : r0 + 1, :]

    moves = []
    for index, (dx, dz) in enumerate(
        ((0, 1), (0, -1), (1, 0), (-1, 0), (1, 1), (1, -1), (-1, 1), (-1, -1))
    ):
        xs = 1 if dx > 0 else 0
        zs = 1 if dz > 0 else 0
        if dx == 0:
            source = rot.at[:, :, pl.ds(ROWS * (ROWS if dz > 0 else 1), ROWS), :]
            target = rot.at[:, :, pl.ds(0 if dz > 0 else ROWS * (ROWS + 1), ROWS), :]
        elif dz == 0:
            source = border.at[xs]
            target = side.at[1 - xs, :, pl.ds(8, ROWS), :]
        else:
            source = corner.at[xs, zs]
            target = near.at[1 - xs, 1 - zs]
        copy = pltpu.make_async_remote_copy(
            src_ref=source, dst_ref=target, send_sem=halo_send.at[index], recv_sem=halo_recv.at[index],
            device_id={"shot": shot + dx, "slab": slab + dz}, device_id_type=MESH,
        )
        goes = (shot + dx >= 0) & (shot + dx < SHOTS) & (slab + dz >= 0) & (slab + dz < SLABS)
        comes = (shot - dx >= 0) & (shot - dx < SHOTS) & (slab - dz >= 0) & (slab - dz < SLABS)
        moves.append((copy, goes, comes, target, dx, dz))

    for copy, goes, comes, target, dx, dz in moves:
        if dz != 0:
            @pl.when(goes)
            def _():
                copy.start()

    def update_both(z, carry):
        update(z, 0)
        update(z, 1)
        return carry

    lax.fori_loop(1, ROWS - 1, update_both, 0)
    for h in range(2):
        ys = slice(h * HALF, (h + 1) * HALF)
        for n in range(3):
            border[0, n, :, ys] = rot[h, n, pl.ds(ROWS, ROWS, stride=ROWS), :]
            border[1, n, :, ys] = rot[h, n, pl.ds(2 * ROWS - 1, ROWS, stride=ROWS), :]

    for copy, goes, comes, target, dx, dz in moves:
        if dz == 0:
            @pl.when(goes)
            def _():
                copy.start()

        if dx != 0:
            @pl.when(jnp.logical_not(comes))
            def _():
                target[...] = jnp.zeros(target.shape, F32)

    for h in range(2):
        @pl.when(ranks[h] < LAST)
        def _():
            pltpu.make_async_copy(held.at[h], held.at[h], stream_send.at[h]).wait()

    @pl.when(is_end)
    def _():
        others = parts.at[:, pl.ds(0, SLABS - 1)]
        pltpu.make_async_copy(others, others, part_send).wait()

    @pl.when(is_end & (chunk_own == shot))
    def _():
        others = product.at[:, pl.ds(0, SLABS - 1)]
        pltpu.make_async_copy(others, others, back_send).wait()

    @pl.when(is_end & (chunk_own != shot))
    def _():
        pltpu.make_async_copy(product, product, back_send).wait()

    for copy, goes, comes, target, dx, dz in moves:
        @pl.when(comes)
        def _():
            copy.wait_recv()

    for s in range(2):
        for n in range(3):
            side[s, n, 7:8, :] = near[s, 0, n : n + 1, :]
            side[s, n, 8 + ROWS : 9 + ROWS, :] = near[s, 1, n : n + 1, :]
            edge[s, n] = (
                0.25 * (side[s, n, 7 : 7 + ROWS, :] + side[s, n, 9 : 9 + ROWS, :]) + 0.5 * side[s, n, 8 : 8 + ROWS, :]
            )

    def average(group, carry):
        x_at = lax.broadcasted_iota(jnp.int32, (ROWS, HALF), 0)
        z0 = pl.multiple_of(group * 8, 8)
        for n in range(3):
            for h in range(2):
                ys = slice(h * HALF, (h + 1) * HALF)
                low = edge[0, n, pl.ds(z0, 8), ys]
                high = edge[1, n, pl.ds(z0, 8), ys]
                for i in range(8):
                    three = [
                        rot[h, n, pl.ds(pl.multiple_of((z0 + i + j) * ROWS, ROWS), ROWS), :] for j in range(3)
                    ]
                    mean = 0.25 * (three[0] + three[2]) + 0.5 * three[1]
                    before = jnp.where(x_at == 0, low[i : i + 1], pltpu.roll(mean, 1, 0))
                    after = jnp.where(x_at == ROWS - 1, high[i : i + 1], pltpu.roll(mean, ROWS - 1, 0))
                    out[n, z0 + i, :, ys] = 0.25 * (before + after) + 0.5 * mean
        return carry

    lax.fori_loop(0, ROWS // 8, average, 0)

    for copy, goes, comes, target, dx, dz in moves:
        @pl.when(goes)
        def _():
            copy.wait_send()


def shards(partial_grads, model, tilt, widths, step_length):
    vmem = pl.BlockSpec(memory_space=pltpu.VMEM)
    hbm = pl.BlockSpec(memory_space=pl.ANY)
    wide = 2 * HALF
    return pl.pallas_call(
        kernel,
        out_shape=jax.ShapeDtypeStruct(model.shape, F32),
        in_specs=[hbm] * 5,
        out_specs=vmem,
        scratch_shapes=[
            pltpu.VMEM(partial_grads.shape[1:], BF16),
            pltpu.VMEM(model.shape, F32),
            pltpu.VMEM(tilt.shape, F32),
            pltpu.VMEM(widths.shape, F32),
            pltpu.SMEM(step_length.shape, F32),
            pltpu.VMEM((2, PIECES, PIECE, ROWS, HALF), BF16),
            pltpu.VMEM((ROWS * ROWS, HALF), F32),
            pltpu.VMEM((3, SLABS, ROWS, wide), BF16),
            pltpu.VMEM((3, NZ, wide), BF16),
            pltpu.VMEM((3, NZ, NZ), BF16),
            pltpu.VMEM((3, SLABS, ROWS, wide), BF16),
            pltpu.VMEM((2, 8, 3, ROWS, wide), BF16),
            pltpu.VMEM((2, 3, ROWS * ROWS, HALF), F32),
            pltpu.VMEM((2, ROWS, ROWS, wide), F32),
            pltpu.VMEM((2, 3, (ROWS + 2) * ROWS, HALF), F32),
            pltpu.VMEM((2, 3, ROWS, wide), F32),
            pltpu.VMEM((2, 2, 8, wide), F32),
            pltpu.VMEM((2, 3, 2 * ROWS, wide), F32),
            pltpu.VMEM((2, 2, 8, wide), F32),
            pltpu.VMEM((2, 3, ROWS, wide), F32),
            pltpu.SemaphoreType.REGULAR,
            pltpu.SemaphoreType.DMA((5,)),
            pltpu.SemaphoreType.DMA((2,)),
            pltpu.SemaphoreType.DMA((2, PIECES)),
            pltpu.SemaphoreType.DMA,
            pltpu.SemaphoreType.DMA((3,)),
            pltpu.SemaphoreType.DMA,
            pltpu.SemaphoreType.DMA((3,)),
            pltpu.SemaphoreType.DMA((8,)),
            pltpu.SemaphoreType.DMA((8,)),
        ],
        compiler_params=pltpu.CompilerParams(
            collective_id=0, has_side_effects=True, vmem_limit_bytes=60 * 1024 * 1024
        ),
    )(partial_grads[0], model, tilt, widths, step_length)


def solution(mesh):
    placed = (
        P("shot", None, "slab", None, None),
        P(None, "slab", "shot", None),
        P("slab", "shot", None),
        P(),
        P(),
    )
    return jax.shard_map(
        shards, mesh=mesh, in_specs=placed, out_specs=P(None, "slab", "shot", None), check_vma=False
    )
```
